512 devices in a mesh: dp: 2 (over y_hi), segment: 8 (over x, core), tile: 32 (over y_lo, z).
Axes of the slice: x: 4, y: 8 (y_hi: 2, y_lo: 4; y = y_hi * 4 + y_lo), z: 8, core: 2. Of those that a mesh axis runs over, the one named last changes fastest.
Arguments:
- inputs: bfloat16 [4, 32, 32, 32, 128], P('dp', 'tile'), may hold values from -6 to 6
- neighbor: int32 [32, 4], replicated, may hold values from 0 to 31, as said below
- edge_of: int32 [32, 4], replicated, may hold values from 0 to 3
- reverse: int32 [32, 4], replicated, may hold values from 0 to 1, as said below
- weights: bfloat16 [8, 1152, 128], P('segment'), may hold values from -0.1875 to 0.1875
- cotangent: bfloat16 [8, 4, 32, 32, 32, 128], P('segment', 'dp', 'tile'), may hold values from -6 to 6
Outputs:
- levels: bfloat16 [8, 4, 32, 32, 32, 128], P('segment', 'dp', 'tile')
- grads: float32 [8, 1152, 128], P('segment')
The draws below stay inside these ranges and needn't reach their ends.
Inputs may be any that keep to these rules, and one draw needn't show every extreme that they name: The seams pair the edges: every (tile, edge) slot is named by exactly one slot, and if (t, d) names (neighbor[t, d], edge_of[t, d]) = (u, e), then (u, e) names (t, d). reverse[t, d] equals reverse at the partner slot (neighbor[t, d], edge_of[t, d]).
All inputs are finite; a program needn't handle non-finite values.
Results may differ from the reference program's by a relative error of at most 0.017.
Values may be sent and summed in bfloat16 or wider, within the bound.
No kernel may reach another device: no remote copies, remote signals or barrier semaphores. Data moves between devices by JAX's collectives and lax.ppermute only.
A program may use at most 64 MiB of HBM per device.

```python
import jax
import jax.numpy as jnp
from jax import lax

C = 128
SIDE = 32
SAMPLES = 4
TILES = 32
SEGMENTS = 8


def seam_pairs(key):
    slots = TILES * 4
    order = jax.random.permutation(jax.random.fold_in(key, 101), slots).astype(jnp.int32)
    first = order[0::2]
    second = order[1::2]
    partner = jnp.zeros((slots,), jnp.int32).at[first].set(second).at[second].set(first)
    bits = jax.random.randint(jax.random.fold_in(key, 102), (slots // 2,), 0, 2).astype(jnp.int32)
    flips = jnp.zeros((slots,), jnp.int32).at[first].set(bits).at[second].set(bits)
    return (partner.reshape(TILES, 4), flips.reshape(TILES, 4))


def draw_neighbor(key, part):
    partner, flips = seam_pairs(key)
    return (partner // 4).astype(jnp.int32)


def draw_edge_of(key, part):
    partner, flips = seam_pairs(key)
    return (partner % 4).astype(jnp.int32)


def draw_reverse(key, part):
    partner, flips = seam_pairs(key)
    return flips.astype(jnp.int32)


def shard_levels(own_key, extent, pieces, smallest, largest):
    gain, own = 1.0, jax.random.fold_in(own_key, 6)
    for dim, blocks in pieces:
        heights = jnp.exp(jax.random.uniform(jax.random.fold_in(own, dim), (blocks,), jnp.float32, smallest / len(pieces), largest / len(pieces)))
        gain = gain * jnp.repeat(heights, extent[dim] // blocks).reshape([-1 if axis == dim else 1 for axis in range(len(extent))])
    return gain


def normal_values(key, dims, scale, bound, pieces=(), held_as=jnp.bfloat16):
    gain = shard_levels(key, dims, pieces, -0.22, 0.18) if pieces else 1.0
    entries = jax.random.normal(key, dims, jnp.float32) * scale * gain
    return jnp.minimum(jnp.maximum(entries, -bound), bound).astype(held_as)


def setup_inputs(seed: int = 0) -> dict:
    seeds = jax.random.split(jax.random.key(seed), 7)
    return {
        "inputs": normal_values(seeds[0], (SAMPLES, TILES, SIDE, SIDE, C), 1.0, 6.0, ((0, 2), (1, 32))),
        "neighbor": draw_neighbor(jax.random.fold_in(seeds[6], 71), 0),
        "edge_of": draw_edge_of(jax.random.fold_in(seeds[6], 71), 0),
        "reverse": draw_reverse(jax.random.fold_in(seeds[6], 71), 0),
        "weights": normal_values(seeds[4], (SEGMENTS, 9 * C, C), (9 * C) ** -0.5, 0.1875, ((0, 8),)),
        "cotangent": normal_values(seeds[5], (SEGMENTS, SAMPLES, TILES, SIDE, SIDE, C), 1.0, 6.0, ((0, 8), (1, 2), (2, 32))),
    }


def make_patches(padded, side):
    parts = []
    for k in range(9):
        dy = k // 3
        dx = k % 3
        parts.append(padded[..., dy:dy + side, dx:dx + side, :])
    return jnp.concatenate(parts, axis=-1)


def silu_slope(value):
    sigma = jax.nn.sigmoid(value)
    return sigma * (1.0 + value * (1.0 - sigma))


def pad_tiles(state, halo):
    corner = jnp.zeros(state.shape[:2] + (1, 1, state.shape[4]), state.dtype)
    top = jnp.concatenate([corner, halo[:, :, 0][:, :, None], corner], axis=3)
    bottom = jnp.concatenate([corner, halo[:, :, 2][:, :, None], corner], axis=3)
    middle = jnp.concatenate([halo[:, :, 3][:, :, :, None], state, halo[:, :, 1][:, :, :, None]], axis=3)
    return jnp.concatenate([top, middle, bottom], axis=2)


def reference(inputs, neighbor, edge_of, reverse, weights, cotangent):
    batch = inputs.shape[0]
    tiles = inputs.shape[1]
    side = inputs.shape[2]
    chans = inputs.shape[4]
    source = (neighbor * 4 + edge_of).reshape(-1).astype(jnp.int32)
    state = inputs
    outputs = []
    kernels = []
    for s in range(SEGMENTS):
        edges = jnp.stack([state[:, :, 0, :, :], state[:, :, :, side - 1, :], state[:, :, side - 1, :, :], state[:, :, :, 0, :]], axis=2)
        flat = edges.reshape(batch, tiles * 4, side, chans)
        halo = flat[:, source].reshape(batch, tiles, 4, side, chans)
        halo = jnp.where(reverse[None, :, :, None, None] == 1, halo[:, :, :, ::-1, :], halo)
        padded = pad_tiles(state, halo)
        patches = make_patches(padded, side).reshape(-1, 9 * chans)
        pre_act = jnp.dot(patches, weights[s], preferred_element_type=jnp.float32)
        flat_state = state.reshape(-1, chans).astype(jnp.float32)
        new_state = (flat_state + jax.nn.silu(pre_act)).astype(jnp.bfloat16)
        delta = (cotangent[s].reshape(-1, chans).astype(jnp.float32) * silu_slope(pre_act)).astype(jnp.bfloat16)
        kernels.append(lax.dot_general(patches, delta, (((0,), (0,)), ((), ())), preferred_element_type=jnp.float32))
        state = new_state.reshape(inputs.shape)
        outputs.append(state)
    return jnp.stack(outputs, axis=0), jnp.stack(kernels, axis=0)
```

```python
import jax
import jax.numpy as jnp
from jax import lax
from jax.sharding import PartitionSpec as P


def from_behind(shard, axis, by):
    count = lax.axis_size(axis)
    pairs = [(i, i + by) for i in range(count) if 0 <= i + by < count]
    return lax.ppermute(shard, axis, pairs)


def make_patches(padded, side):
    parts = []
    for k in range(9):
        dy = k // 3
        dx = k % 3
        parts.append(padded[dy : dy + side, dx : dx + side, :])
    return jnp.concatenate(parts, axis=-1)


def silu_slope(value):
    sigma = jax.nn.sigmoid(value)
    return sigma * (1.0 + value * (1.0 - sigma))


def pad_tile(state, strips):
    corner = jnp.zeros((1, 1, state.shape[2]), state.dtype)
    top = jnp.concatenate([corner, strips[0][None], corner], axis=1)
    bottom = jnp.concatenate([corner, strips[2][None], corner], axis=1)
    middle = jnp.concatenate([strips[3][:, None], state, strips[1][:, None]], axis=1)
    return jnp.concatenate([top, middle, bottom], axis=0)


def sum_terms(term):
    axes = ("dp", "tile")
    count = lax.axis_size(axes)
    rows = term.shape[0] // count
    pieces = term.astype(jnp.bfloat16).reshape(count, rows, term.shape[1])
    pieces = lax.all_to_all(pieces, axes, 0, 0)
    piece = jnp.sum(pieces.astype(jnp.float32), axis=0).astype(jnp.bfloat16)
    pieces = lax.all_to_all(jnp.broadcast_to(piece[None], pieces.shape), axes, 0, 0)
    return pieces.reshape(term.shape).astype(jnp.float32)


def local(inputs, neighbor, edge_of, reverse, weights, cotangent):
    samples = inputs.shape[0]
    side = inputs.shape[2]
    chans = inputs.shape[4]
    segment_count = lax.axis_size("segment")
    segment = lax.axis_index("segment")
    tile = lax.axis_index("tile")
    source = lax.dynamic_index_in_dim(neighbor, tile, 0, False) * 4 + lax.dynamic_index_in_dim(
        edge_of, tile, 0, False
    )
    flips = lax.dynamic_index_in_dim(reverse, tile, 0, False)
    kernel = weights[0]
    firsts = inputs[:, 0]
    cotans = cotangent[0, :, 0]

    def seam_strips(state):
        edges = jnp.stack(
            [state[0, :, :], state[:, side - 1, :], state[side - 1, :, :], state[:, 0, :]], axis=0
        )[None]
        tiles = lax.axis_size("tile")
        copies = jnp.broadcast_to(edges, (tiles,) + edges.shape[1:])
        gathered = lax.all_to_all(copies, "tile", 0, 0)
        count = gathered.shape[0] * 4
        onehot = (source[:, None] == jnp.arange(count, dtype=jnp.int32)[None, :]).astype(
            jnp.bfloat16
        )
        picked = jnp.dot(
            onehot, gathered.reshape(count, side * chans), preferred_element_type=jnp.float32
        )
        strips = picked.astype(jnp.bfloat16).reshape(4, side, chans)
        return jnp.where(flips[:, None, None] == 1, strips[:, ::-1, :], strips)

    def tick(step, carry):
        current, outputs, kernel_sum = carry
        index = step - segment
        valid = (index >= 0) & (index < samples)
        clipped = jnp.clip(index, 0, samples - 1)
        first = lax.dynamic_index_in_dim(firsts, clipped, 0, False)
        state = jnp.where(segment == 0, first, current)
        strips = seam_strips(state)
        padded = pad_tile(state, strips)
        patches = make_patches(padded, side).reshape(side * side, 9 * chans)
        pre_act = jnp.dot(patches, kernel, preferred_element_type=jnp.float32)
        new_flat = (
            state.reshape(side * side, chans).astype(jnp.float32) + jax.nn.silu(pre_act)
        ).astype(jnp.bfloat16)
        new_state = new_flat.reshape(side, side, chans)
        cotan = lax.dynamic_index_in_dim(cotans, clipped, 0, False).reshape(side * side, chans)
        delta = (cotan.astype(jnp.float32) * silu_slope(pre_act)).astype(jnp.bfloat16)
        term = lax.dot_general(
            patches, delta, (((0,), (0,)), ((), ())), preferred_element_type=jnp.float32
        )
        kernel_sum = kernel_sum + jnp.where(valid, term, jnp.zeros_like(term))
        previous = lax.dynamic_index_in_dim(outputs, clipped, 0, False)
        outputs = lax.dynamic_update_index_in_dim(
            outputs, jnp.where(valid, new_state, previous), clipped, 0
        )
        current = from_behind(new_state, "segment", 1)
        return (current, outputs, kernel_sum)

    start = (
        jnp.zeros((side, side, chans), jnp.bfloat16),
        jnp.zeros((samples, side, side, chans), jnp.bfloat16),
        jnp.zeros((9 * chans, chans), jnp.float32),
    )
    current, outputs, kernel_sum = lax.fori_loop(0, samples + segment_count - 1, tick, start)
    total = sum_terms(kernel_sum)
    return (outputs[None, :, None], total[None])


def solution(mesh):
    placed = (
        P("dp", "tile", None, None, None),
        P(),
        P(),
        P(),
        P("segment", None, None),
        P("segment", "dp", "tile", None, None, None),
    )
    return jax.shard_map(
        local,
        mesh=mesh,
        in_specs=placed,
        out_specs=(P("segment", "dp", "tile", None, None, None), P("segment", None, None)),
        check_vma=False,
    )
```

```python
import jax
import jax.numpy as jnp
from jax import lax
from jax.experimental import pallas as pl
from jax.experimental.pallas import tpu as pltpu
from jax.sharding import PartitionSpec as P

SIDE = 32
CELLS = SIDE * SIDE
RING = 4 * SIDE
C = 128
TAPS = 9
SPLIT = 4
PART = SIDE // SPLIT
PICK = 8 * PART + 16
VMEM_BYTES = 40 * 1024 * 1024


def iota(shape, axis):
    return lax.broadcasted_iota(jnp.int32, shape, axis)


def onehot(target, columns):
    return (target[:, None] == iota((target.shape[0], columns), 1)).astype(jnp.bfloat16)


def lookup(table, index):
    flat = table.reshape(-1)
    hit = index[..., None] == jnp.arange(flat.shape[0], dtype=jnp.int32)
    return jnp.sum(jnp.where(hit, flat, 0), axis=-1)


def rim_cell(edge, depth, place):
    last = SIDE - 1
    return jnp.where(
        edge == 0,
        depth * SIDE + place,
        jnp.where(
            edge == 1,
            place * SIDE + last - depth,
            jnp.where(edge == 2, (last - depth) * SIDE + place, place * SIDE + depth),
        ),
    )


def selections(neighbor, edge_of, reverse, tile, part):
    d4 = jnp.arange(4, dtype=jnp.int32)
    own = tile * 4 + d4
    nbr, edge, flip = lookup(neighbor, own), lookup(edge_of, own), lookup(reverse, own)
    tiles = neighbor.shape[0]
    row = jnp.arange(8 * PART, dtype=jnp.int32)
    share = rim_cell(row // (2 * PART), row // PART % 2, part * PART + row % PART)
    rim = onehot(share, CELLS)
    width = 8 * PART
    row = jnp.arange(8 * PART, dtype=jnp.int32)
    d = row // (2 * PART)
    strips = lookup(nbr, d) * width + lookup(edge, d) * (2 * PART) + row % (2 * PART)
    row = jnp.arange(16, dtype=jnp.int32)
    d, end, depth = row // 4, row // 2 % 2, row % 2
    e = lookup(edge, d)
    side = jnp.where(e % 2 == 0, 3 - 2 * end, 2 * end)
    slot = lookup(nbr, d) * 4 + side
    place = jnp.where((e == 0) | (e == 3), depth, SIDE - 1 - depth)
    place = jnp.where(lookup(reverse, slot) == 1, SIDE - 1 - place, place)
    ends = lookup(neighbor, slot) * width + lookup(edge_of, slot) * (2 * PART) + place % PART
    ends = jnp.where(place // PART == part, ends, -1)
    pick = onehot(jnp.concatenate([strips, ends]), tiles * width)
    row = jnp.arange(RING, dtype=jnp.int32)
    d, place = row // SIDE, row % SIDE
    turned = jnp.where(lookup(flip, d) == 1, SIDE - 1 - place, place)

    def picked(where, depth):
        return where // PART * PICK + d * (2 * PART) + depth * PART + where % PART

    end = jnp.where(place == 0, 0, jnp.where(place == SIDE - 1, 1, -1))
    column = iota((RING, SPLIT * PICK), 1) % PICK

    def beyond(depth):
        target = jnp.where(end < 0, -1, 8 * PART + d * 4 + end * 2 + depth)
        return (target[:, None] == column).astype(jnp.bfloat16)

    ring = jnp.concatenate(
        [
            onehot(picked(turned, 0), SPLIT * PICK),
            onehot(picked(place, 0), SPLIT * PICK),
            onehot(picked(place, 1), SPLIT * PICK),
            beyond(0),
            beyond(1),
        ]
    )
    facing = onehot(rim_cell(d, 0, turned), CELLS)
    turn = onehot(d * SIDE + turned, RING)
    return edge, rim, pick, ring, facing, turn


def sigmoid(value):
    return 1.0 / (1.0 + jnp.exp(-value))


def fill_patches(state, padded, patches):
    padded[1 : SIDE + 1, 8 : SIDE + 8, :] = (
        state[0:CELLS, :].astype(jnp.float32).reshape(SIDE, SIDE, C)
    )
    halo = state[CELLS : CELLS + RING, :].astype(jnp.float32)
    empty = jnp.zeros((8, C), jnp.float32)
    for row, first in ((0, 0), (SIDE + 1, 2 * SIDE)):
        padded[row, 0:8, :] = empty
        padded[row, 8 : SIDE + 8, :] = halo[first : first + SIDE]
        padded[row, SIDE + 8 : SIDE + 16, :] = empty
    padded[1 : SIDE + 1, SIDE + 8, :] = halo[SIDE : 2 * SIDE]
    padded[1 : SIDE + 1, 7, :] = halo[3 * SIDE : 4 * SIDE]
    for dx in range(3):
        shifted = padded[:, 7 + dx : 7 + dx + SIDE, :].astype(jnp.bfloat16)
        shifted = shifted.reshape((SIDE + 2) * SIDE, C)
        for dy in range(3):
            k = dy * 3 + dx
            patches[:, k * C : (k + 1) * C] = shifted[dy * SIDE : dy * SIDE + CELLS]


def next_state(state, pre_act):
    return (state + pre_act * sigmoid(pre_act)).astype(jnp.bfloat16)


def dot(a, b):
    return jnp.dot(a, b, preferred_element_type=jnp.float32)


def round_kernel(
    edge, start, gathered, weights, rim, ring, facing, turn, first, second, out, share, padded, patches, side_patches
):
    strips = dot(ring[...], gathered[...])
    first[0:CELLS, :] = start[...]
    first[CELLS : CELLS + RING, :] = strips[0:RING].astype(jnp.bfloat16)
    near, far = strips[RING : 2 * RING], strips[2 * RING : 3 * RING]
    near_ends, far_ends = strips[3 * RING : 4 * RING], strips[4 * RING : 5 * RING]
    mine = dot(facing[...], start[...])
    place = iota((RING, C), 0) % SIDE
    for a, (cells, ends) in enumerate(((mine, jnp.zeros_like(mine)), (near, near_ends), (far, far_ends))):
        below = jnp.where(place == 0, ends, pltpu.roll(cells, 1, 0))
        above = jnp.where(place == SIDE - 1, ends, pltpu.roll(cells, RING - 1, 0))
        for b, moved in enumerate((below, cells, above)):
            moved = moved.astype(jnp.bfloat16)
            for d in range(4):
                e = edge[d]
                across = jnp.where((e == 0) | (e == 3), a, 2 - a)
                tap = jnp.where(e % 2 == 0, 3 * across + b, 3 * b + across)
                side_patches[d * SIDE : (d + 1) * SIDE, pl.ds(pl.multiple_of(tap * C, C), C)] = moved[
                    d * SIDE : (d + 1) * SIDE
                ]
    new_side = next_state(near, dot(side_patches[...], weights[0]))
    fill_patches(first, padded, patches)
    second[0:CELLS, :] = next_state(start[...].astype(jnp.float32), dot(patches[...], weights[0]))
    second[CELLS : CELLS + RING, :] = dot(turn[...], new_side).astype(jnp.bfloat16)
    fill_patches(second, padded, patches)
    new = next_state(second[0:CELLS, :].astype(jnp.float32), dot(patches[...], weights[1]))
    out[...] = new
    share[...] = dot(rim[...], new).astype(jnp.bfloat16)


def two_sections(edge, start, gathered, weights, rim, ring, facing, turn):
    vmem = pl.BlockSpec(memory_space=pltpu.VMEM)
    bf16 = jnp.bfloat16
    return pl.pallas_call(
        round_kernel,
        out_shape=(
            jax.ShapeDtypeStruct((CELLS + RING, C), bf16),
            jax.ShapeDtypeStruct((CELLS + RING, C), bf16),
            jax.ShapeDtypeStruct((CELLS, C), bf16),
            jax.ShapeDtypeStruct((8 * PART, C), bf16),
        ),
        in_specs=[pl.BlockSpec(memory_space=pltpu.SMEM)] + [vmem] * 7,
        out_specs=(vmem,) * 4,
        scratch_shapes=[
            pltpu.VMEM((SIDE + 2, SIDE + 16, C), jnp.float32),
            pltpu.VMEM((CELLS, TAPS * C), bf16),
            pltpu.VMEM((RING, TAPS * C), bf16),
        ],
        compiler_params=pltpu.CompilerParams(vmem_limit_bytes=VMEM_BYTES),
        cost_estimate=pl.CostEstimate(
            flops=2 * 2 * CELLS * TAPS * C * C, bytes_accessed=4 << 20, transcendentals=2 * CELLS * C
        ),
        name="two_sections",
    )(edge, start, gathered, weights, rim, ring, facing, turn)


def choose_kernel(index, *refs):
    states, (kept, sent), sems = refs[:8], refs[8:10], refs[10]
    for slot, target in ((0, kept), (1, sent)):
        for s in range(8):

            @pl.when(index[slot] == s)
            def _(s=s, slot=slot, target=target):
                copy = pltpu.make_async_copy(states[s], target, sems.at[slot])
                copy.start()
                copy.wait()


def choose(index, states):
    shape = jax.ShapeDtypeStruct(states[0].shape, states[0].dtype)
    return pl.pallas_call(
        choose_kernel,
        out_shape=(shape, shape),
        in_specs=[pl.BlockSpec(memory_space=pltpu.SMEM)] + [pl.BlockSpec(memory_space=pl.ANY)] * 8,
        out_specs=(pl.BlockSpec(memory_space=pl.ANY),) * 2,
        scratch_shapes=[pltpu.SemaphoreType.DMA((2,))],
        name="choose",
    )(index, *states)


def gradient_kernel(state, cotangent, weights, before, level, term, padded, patches):
    fill_patches(state, padded, patches)
    pre_act = dot(patches[...], weights[...])
    gate = sigmoid(pre_act)
    level[...] = (state[0:CELLS, :].astype(jnp.float32) + pre_act * gate).astype(jnp.bfloat16)
    slope = gate * (1.0 + pre_act * (1.0 - gate))
    delta = (cotangent[...].astype(jnp.float32) * slope).astype(jnp.bfloat16)
    added = lax.dot_general(
        patches[...], delta, (((0,), (0,)), ((), ())), preferred_element_type=jnp.float32
    )
    term[...] = (before[...] + added).astype(term.dtype)


def gradient(state, cotangent, weights, before, dtype):
    vmem = pl.BlockSpec(memory_space=pltpu.VMEM)
    return pl.pallas_call(
        gradient_kernel,
        out_shape=(
            jax.ShapeDtypeStruct((CELLS, C), jnp.bfloat16),
            jax.ShapeDtypeStruct((TAPS * C, C), dtype),
        ),
        in_specs=[vmem] * 4,
        out_specs=(vmem,) * 2,
        scratch_shapes=[
            pltpu.VMEM((SIDE + 2, SIDE + 16, C), jnp.float32),
            pltpu.VMEM((CELLS, TAPS * C), jnp.bfloat16),
        ],
        compiler_params=pltpu.CompilerParams(vmem_limit_bytes=VMEM_BYTES),
        cost_estimate=pl.CostEstimate(
            flops=2 * 2 * CELLS * TAPS * C * C, bytes_accessed=3 << 20, transcendentals=CELLS * C
        ),
        name="gradient",
    )(state, cotangent, weights, before)


def share_out(block, axis, groups=None):
    count = lax.axis_size(axis) if groups is None else len(groups[0])
    return lax.all_to_all(
        jnp.broadcast_to(block[None], (count,) + block.shape), axis, 0, 0, axis_index_groups=groups
    )


def sum_terms(term):
    axes = ("dp", "tile")
    count = lax.axis_size(axes)
    rows = term.shape[0] // count
    pieces = lax.all_to_all(term.reshape(count, rows, term.shape[1]), axes, 0, 0)
    piece = jnp.sum(pieces.astype(jnp.float32), axis=0).astype(jnp.bfloat16)
    return share_out(piece, axes).reshape(term.shape).astype(jnp.float32)


def local(inputs, neighbor, edge_of, reverse, weights, cotangent):
    segment = lax.axis_index("segment")
    sample, part = segment // SPLIT, segment % SPLIT
    teams = [[t * SPLIT + p for p in range(SPLIT)] for t in range(2)]
    kernels = lax.all_gather(weights, "segment", axis=0, tiled=True)
    edge, rim, pick, ring, facing, turn = selections(
        neighbor, edge_of, reverse, lax.axis_index("tile"), part
    )
    state = lax.dynamic_index_in_dim(inputs[:, 0], sample, 0, False).reshape(CELLS, C)
    share = dot(rim, state).astype(jnp.bfloat16)
    states = []
    for step in range(4):
        rims = share_out(share, "tile").reshape(-1, C)
        picked = dot(pick, rims).astype(jnp.bfloat16)
        gathered = share_out(picked, "segment", teams).reshape(-1, C)
        pair = kernels[2 * step : 2 * step + 2]
        first, second, state, share = two_sections(edge, state, gathered, pair, rim, ring, facing, turn)
        states += [first, second]
    partner = segment ^ SPLIT
    kept, sent = choose(jnp.stack([segment, partner]).astype(jnp.int32), states)
    other = lax.ppermute(sent, "segment", [(s, s ^ SPLIT) for s in range(8)])
    cotans = cotangent[0, :, 0].reshape(2, CELLS, C)
    mine = lax.dynamic_index_in_dim(cotans, sample, 0, False)
    theirs = lax.dynamic_index_in_dim(cotans, 1 - sample, 0, False)
    zero = jnp.zeros((TAPS * C, C), jnp.float32)
    level_mine, term = gradient(kept, mine, weights[0], zero, jnp.float32)
    level_other, term = gradient(other, theirs, weights[0], term, jnp.bfloat16)
    total = sum_terms(term)
    low = jnp.where(sample == 0, level_mine, level_other)
    high = jnp.where(sample == 0, level_other, level_mine)
    levels = jnp.stack([low, high]).reshape(1, 2, 1, SIDE, SIDE, C)
    return levels, total[None]


def solution(mesh):
    placed = (
        P("dp", "tile", None, None, None),
        P(),
        P(),
        P(),
        P("segment", None, None),
        P("segment", "dp", "tile", None, None, None),
    )
    return jax.shard_map(
        local,
        mesh=mesh,
        in_specs=placed,
        out_specs=(P("segment", "dp", "tile", None, None, None), P("segment", None, None)),
        check_vma=False,
    )
```

```python
import jax
import jax.numpy as jnp
from jax import lax
from jax.experimental import pallas as pl
from jax.experimental.pallas import tpu as pltpu
from jax.sharding import PartitionSpec as P

SIDE = 32
CELLS = SIDE * SIDE
RING = 4 * SIDE
C = 128
TAPS = 9
DEPTH = 4
SPLIT = 4
PART = SIDE // SPLIT
EDGE = DEPTH * PART
SHARE = 4 * EDGE
BLOCKS = [[(x, c) for x in range(DEPTH + 1 - j) for c in range(DEPTH - j)] for j in range(1, DEPTH)]
SLOTS = sum(len(block) for block in BLOCKS)
FANS = 8
PICK = SHARE + FANS * SLOTS
VMEM_BYTES = 48 * 1024 * 1024


def iota(shape, axis):
    return lax.broadcasted_iota(jnp.int32, shape, axis)


def onehot(target, columns):
    return (target[:, None] == iota((target.shape[0], columns), 1)).astype(jnp.bfloat16)


def lookup(table, index):
    flat = table.reshape(-1)
    hit = index[..., None] == jnp.arange(flat.shape[0], dtype=jnp.int32)
    return jnp.sum(jnp.where(hit, flat, 0), axis=-1)


def rim_cell(edge, depth, place):
    last = SIDE - 1
    return jnp.where(
        edge == 0,
        depth * SIDE + place,
        jnp.where(
            edge == 1,
            place * SIDE + last - depth,
            jnp.where(edge == 2, (last - depth) * SIDE + place, place * SIDE + depth),
        ),
    )


def walk(tables, tile, edge, end):
    neighbor, edge_of, reverse = tables
    slot = tile * 4 + jnp.where(edge % 2 == 0, 3 - 2 * end, 2 * end)
    corner = jnp.where((edge == 0) | (edge == 3), 0, 1)
    corner = jnp.where(lookup(reverse, slot) == 1, 1 - corner, corner)
    return lookup(neighbor, slot), lookup(edge_of, slot), corner


def spread(columns, counts):
    return jnp.concatenate(
        [jnp.broadcast_to(col[:, None], (FANS, n)) for col, n in zip(columns, counts)], axis=1
    )


def static(values):
    row = jnp.zeros((len(values),), jnp.int32)
    for i, value in enumerate(values):
        row = jnp.where(jnp.arange(len(values), dtype=jnp.int32) == i, value, row)
    return row


def tap_columns(edges, ends, block_of, x, c):
    k = iota((TAPS, 1, 1), 0)
    dy, dx = k // 3 - 1, k % 3 - 1
    edges, ends = edges[None], ends[None]
    down = jnp.where(edges == 0, dy, jnp.where(edges == 2, -dy, jnp.where(edges == 3, dx, -dx)))
    along = jnp.where(edges % 2 == 0, dx, dy)
    along = jnp.where(ends == 1, -along, along)
    return x + along, c + down


def selections(neighbor, edge_of, reverse, tile, part):
    tables = (neighbor, edge_of, reverse)
    own = tile * 4 + jnp.arange(4, dtype=jnp.int32)
    nbr, edge, flip = lookup(neighbor, own), lookup(edge_of, own), lookup(reverse, own)
    tiles = neighbor.shape[0]
    row = jnp.arange(SHARE, dtype=jnp.int32)
    share = rim_cell(row // EDGE, row // PART % DEPTH, part * PART + row % PART)
    rim = onehot(share, CELLS)
    fan = jnp.arange(FANS, dtype=jnp.int32)
    chain = [(lookup(nbr, fan // 2), lookup(edge, fan // 2), fan % 2)]
    for j in range(1, DEPTH):
        chain.append(walk(tables, *chain[-1]))
    around, edges, ends = zip(*chain[1:])
    strips = lookup(nbr, row // EDGE) * SHARE + lookup(edge, row // EDGE) * EDGE + row % EDGE
    counts = [len(block) for block in BLOCKS]
    x = static([cell[0] for block in BLOCKS for cell in block])
    c = static([cell[1] for block in BLOCKS for cell in block])
    place = jnp.where(spread(ends, counts) == 1, SIDE - 1 - x, x)
    cells = spread(around, counts) * SHARE + spread(edges, counts) * EDGE + c * PART + place % PART
    cells = jnp.where(place // PART == part, cells, -1)
    pick = onehot(jnp.concatenate([strips, cells.reshape(-1)]), tiles * SHARE)
    d, place = row // SIDE, row % SIDE
    end = jnp.where(place == 0, 0, jnp.where(place == SIDE - 1, 1, -1))
    beyond = []
    for slots, stride, rows in ((SLOTS, 3, 4), (8, 2, 3), (2, 1, 2)):
        target = (d * 2 + end)[None] * slots + stride * jnp.arange(rows, dtype=jnp.int32)[:, None]
        target = jnp.where(end[None] < 0, -1, target)
        beyond.append(onehot(target.reshape(-1), FANS * slots))
    fan3 = iota((1, FANS, 1), 1)
    at_end = fan3 // 2 * SIDE + fan3 % 2 * (SIDE - 1)
    x = static([0, 0, 1, 1, 2, 2, 0, 1])
    c = static([0, 1, 0, 1, 0, 1, 0, 0])
    near = jnp.arange(8, dtype=jnp.int32) < 6
    x, c = tap_columns(spread(edges[:2], (6, 2)), spread(ends[:2], (6, 2)), near, x, c)
    base = DEPTH * RING + fan3 * SLOTS
    first = jnp.where(
        c < 0,
        jnp.where(near, x * RING + at_end, base + x),
        jnp.where(
            x < 0,
            jnp.where(near, base + 12 + 2 * c, base + 18 + c),
            jnp.where(near, base + 3 * x + c, base + 12 + 2 * x + c),
        ),
    )
    first = onehot(jnp.where((c < 0) & (x < 0), -1, first).reshape(-1), DEPTH * RING + FANS * SLOTS)
    x, c = tap_columns(spread(edges[:1], (2,)), spread(ends[:1], (2,)), None, static([0, 1]), static([0, 0]))
    base = (DEPTH - 1) * RING + fan3 * 8
    second = jnp.where(c < 0, x * RING + at_end, jnp.where(x < 0, base + 6 + c, base + 2 * x + c))
    second = onehot(jnp.where((c < 0) & (x < 0), -1, second).reshape(-1), (DEPTH - 1) * RING + FANS * 8)
    turned = jnp.where(lookup(flip, d) == 1, SIDE - 1 - place, place)
    facing = onehot(rim_cell(d, 0, turned), CELLS)
    turn = onehot(d * SIDE + turned, RING)
    return edge, rim, pick, (*beyond, first, second, facing, turn)


def sigmoid(value):
    return 1.0 / (1.0 + jnp.exp(-value))


def fill_patches(state, padded, patches):
    padded[1 : SIDE + 1, 8 : SIDE + 8, :] = (
        state[0:CELLS, :].astype(jnp.float32).reshape(SIDE, SIDE, C)
    )
    halo = state[CELLS : CELLS + RING, :].astype(jnp.float32)
    empty = jnp.zeros((8, C), jnp.float32)
    for row, first in ((0, 0), (SIDE + 1, 2 * SIDE)):
        padded[row, 0:8, :] = empty
        padded[row, 8 : SIDE + 8, :] = halo[first : first + SIDE]
        padded[row, SIDE + 8 : SIDE + 16, :] = empty
    padded[1 : SIDE + 1, SIDE + 8, :] = halo[SIDE : 2 * SIDE]
    padded[1 : SIDE + 1, 7, :] = halo[3 * SIDE : 4 * SIDE]
    for dx in range(3):
        shifted = padded[:, 7 + dx : 7 + dx + SIDE, :].astype(jnp.bfloat16)
        shifted = shifted.reshape((SIDE + 2) * SIDE, C)
        for dy in range(3):
            k = dy * 3 + dx
            patches[:, k * C : (k + 1) * C] = shifted[dy * SIDE : dy * SIDE + CELLS]


def next_state(state, pre_act):
    return (state + pre_act * sigmoid(pre_act)).astype(jnp.bfloat16)


def dot(a, b):
    return jnp.dot(a, b, preferred_element_type=jnp.float32)


def update_strips(edge, level, strips, ends, mine, weights, side_patches):
    rows = len(strips) - 1
    place = iota((RING, C), 0) % SIDE
    moved = []
    for cells, beyond in [(mine, jnp.zeros_like(mine))] + list(zip(strips, ends)):
        below = jnp.where(place == 0, beyond, pltpu.roll(cells, 1, 0))
        above = jnp.where(place == SIDE - 1, beyond, pltpu.roll(cells, RING - 1, 0))
        moved.append([v.astype(jnp.bfloat16) for v in (below, cells, above)])
    for d in range(4):
        e = edge[d]
        for a in range(3):
            across = jnp.where((e == 0) | (e == 3), a, 2 - a)
            for b in range(3):
                tap = jnp.where(e % 2 == 0, 3 * across + b, 3 * b + across)
                lanes = pl.ds(pl.multiple_of(tap * C, C), C)
                for r in range(rows):
                    first = r * RING + d * SIDE
                    side_patches[first : first + SIDE, lanes] = moved[r + a][b][d * SIDE : (d + 1) * SIDE]
    before = jnp.concatenate(strips[:rows], axis=0)
    after = next_state(before, dot(side_patches[0 : rows * RING, :], weights)).astype(jnp.float32)
    return [after[r * RING : (r + 1) * RING] for r in range(rows)]


def update_fans(taps, strips, fans, weights):
    pool = jnp.concatenate([v.astype(jnp.bfloat16) for v in strips + [fans]], axis=0)
    found = dot(taps[...], pool)
    n = found.shape[0] // TAPS
    parts = [found[k * n : (k + 1) * n] for k in range(TAPS)]
    side = jnp.concatenate([v.astype(jnp.bfloat16) for v in parts], axis=1)
    return next_state(parts[4], dot(side, weights)).astype(jnp.float32)


def round_kernel(step, last, *refs):
    index, edge, start, gathered, all_weights, rim, e0, e1, e2, taps1, taps2, facing, turn = refs[:13]
    refs = refs[13 + (2 if step else 0) :]
    (kept, sent), refs = refs[:2], refs[2:]
    if not last:
        (out, share), refs = refs[:2], refs[2:]
    states, padded, patches, side_patches, weights, weight_sems, sems = refs
    loads = [
        pltpu.make_async_copy(all_weights.at[step * DEPTH + i], weights.at[i], weight_sems.at[i])
        for i in range(DEPTH)
    ]
    for load in loads:
        load.start()
    states[0, 0:CELLS, :] = start[...]
    cells = gathered[...].astype(jnp.float32)
    strips = [
        jnp.concatenate(
            [
                cells[q * PICK + d * EDGE + r * PART : q * PICK + d * EDGE + (r + 1) * PART]
                for d in range(4)
                for q in range(SPLIT)
            ],
            axis=0,
        )
        for r in range(DEPTH)
    ]
    fans = cells[SHARE:PICK]
    for q in range(1, SPLIT):
        fans = fans + cells[q * PICK + SHARE : (q + 1) * PICK]

    def deliver(i, act):
        for slot, target in ((0, kept), (1, sent)):

            @pl.when(index[slot] == step * DEPTH + i)
            def _():
                act(pltpu.make_async_copy(states.at[i], target, sems.at[slot]))

    for i in range(DEPTH):
        state = states.at[i]
        state[CELLS : CELLS + RING, :] = dot(turn[...], strips[0].astype(jnp.bfloat16)).astype(jnp.bfloat16)
        deliver(i, lambda copy: copy.start())
        tile = state[0:CELLS, :]
        if not (last and i == DEPTH - 1):
            fill_patches(state, padded, patches)
        loads[i].wait()
        if i < DEPTH - 1:
            ends = dot((e0, e1, e2)[i][...], fans.astype(jnp.bfloat16))
            ends = [ends[r * RING : (r + 1) * RING] for r in range(DEPTH - i)]
            mine = dot(facing[...], tile)
            moved = update_strips(edge, i, strips, ends, mine, weights[i], side_patches)
            if i < DEPTH - 2:
                fans = update_fans((taps1, taps2)[i], strips, fans, weights[i])
            strips = moved
        if not (last and i == DEPTH - 1):
            new = next_state(tile.astype(jnp.float32), dot(patches[...], weights[i]))
            if i < DEPTH - 1:
                states[i + 1, 0:CELLS, :] = new
            else:
                out[...] = new
                share[...] = dot(rim[...], new).astype(jnp.bfloat16)
    for i in range(DEPTH):
        deliver(i, lambda copy: copy.wait())


def four_sections(step, index, edge, start, gathered, weights, rim, maps, chosen):
    last = step == 1
    vmem = pl.BlockSpec(memory_space=pltpu.VMEM)
    smem = pl.BlockSpec(memory_space=pltpu.SMEM)
    hbm = pl.BlockSpec(memory_space=pl.ANY)
    bf16 = jnp.bfloat16
    state = jax.ShapeDtypeStruct((CELLS + RING, C), bf16)
    outs = [state, state]
    if not last:
        outs += [jax.ShapeDtypeStruct((CELLS, C), bf16), jax.ShapeDtypeStruct((SHARE, C), bf16)]
    return pl.pallas_call(
        lambda *refs: round_kernel(step, last, *refs),
        out_shape=outs,
        in_specs=[smem] * 2 + [vmem] * 2 + [hbm] + [vmem] * 8 + [hbm] * len(chosen),
        out_specs=[hbm] * 2 + [vmem] * (len(outs) - 2),
        scratch_shapes=[
            pltpu.VMEM((DEPTH, CELLS + RING, C), bf16),
            pltpu.VMEM((SIDE + 2, SIDE + 16, C), jnp.float32),
            pltpu.VMEM((CELLS, TAPS * C), bf16),
            pltpu.VMEM(((DEPTH - 1) * RING, TAPS * C), bf16),
            pltpu.VMEM((DEPTH, TAPS * C, C), bf16),
            pltpu.SemaphoreType.DMA((DEPTH,)),
            pltpu.SemaphoreType.DMA((2,)),
        ],
        input_output_aliases={13 + i: i for i in range(len(chosen))},
        compiler_params=pltpu.CompilerParams(vmem_limit_bytes=VMEM_BYTES),
        cost_estimate=pl.CostEstimate(
            flops=2 * DEPTH * CELLS * TAPS * C * C, bytes_accessed=6 << 20, transcendentals=DEPTH * CELLS * C
        ),
        name="four_sections",
    )(index, edge, start, gathered, weights, rim, *maps, *chosen)


def gradient_kernel(state, cotangent, weights, before, level, term, padded, patches):
    fill_patches(state, padded, patches)
    pre_act = dot(patches[...], weights[...])
    gate = sigmoid(pre_act)
    level[...] = (state[0:CELLS, :].astype(jnp.float32) + pre_act * gate).astype(jnp.bfloat16)
    slope = gate * (1.0 + pre_act * (1.0 - gate))
    delta = (cotangent[...].astype(jnp.float32) * slope).astype(jnp.bfloat16)
    added = lax.dot_general(
        patches[...], delta, (((0,), (0,)), ((), ())), preferred_element_type=jnp.float32
    )
    term[...] = (before[...] + added).astype(term.dtype)


def gradient(state, cotangent, weights, before, dtype):
    vmem = pl.BlockSpec(memory_space=pltpu.VMEM)
    return pl.pallas_call(
        gradient_kernel,
        out_shape=(
            jax.ShapeDtypeStruct((CELLS, C), jnp.bfloat16),
            jax.ShapeDtypeStruct((TAPS * C, C), dtype),
        ),
        in_specs=[vmem] * 4,
        out_specs=(vmem,) * 2,
        scratch_shapes=[
            pltpu.VMEM((SIDE + 2, SIDE + 16, C), jnp.float32),
            pltpu.VMEM((CELLS, TAPS * C), jnp.bfloat16),
        ],
        compiler_params=pltpu.CompilerParams(vmem_limit_bytes=VMEM_BYTES),
        cost_estimate=pl.CostEstimate(
            flops=2 * 2 * CELLS * TAPS * C * C, bytes_accessed=3 << 20, transcendentals=CELLS * C
        ),
        name="gradient",
    )(state, cotangent, weights, before)


def share_out(block, axis, groups=None):
    count = lax.axis_size(axis) if groups is None else len(groups[0])
    return lax.all_to_all(
        jnp.broadcast_to(block[None], (count,) + block.shape), axis, 0, 0, axis_index_groups=groups
    )


def sum_terms(term):
    axes = ("dp", "tile")
    count = lax.axis_size(axes)
    rows = term.shape[0] // count
    pieces = lax.all_to_all(term.reshape(count, rows, term.shape[1]), axes, 0, 0)
    piece = jnp.sum(pieces.astype(jnp.float32), axis=0).astype(jnp.bfloat16)
    return share_out(piece, axes).reshape(term.shape).astype(jnp.float32)


def local(inputs, neighbor, edge_of, reverse, weights, cotangent):
    segment = lax.axis_index("segment")
    sample, part = segment // SPLIT, segment % SPLIT
    partner = segment ^ SPLIT
    teams = [[t * SPLIT + p for p in range(SPLIT)] for t in range(2)]
    kernels = lax.all_gather(weights, "segment", axis=0, tiled=True)
    edge, rim, pick, maps = selections(neighbor, edge_of, reverse, lax.axis_index("tile"), part)
    index = jnp.stack([segment, partner]).astype(jnp.int32)
    state = lax.dynamic_index_in_dim(inputs[:, 0], sample, 0, False).reshape(CELLS, C)
    share = dot(rim, state).astype(jnp.bfloat16)
    chosen = ()
    for step in range(2):
        rims = share_out(share, "tile").reshape(-1, C)
        picked = dot(pick, rims).astype(jnp.bfloat16)
        gathered = lax.all_gather(picked, "segment", axis=0, tiled=True, axis_index_groups=teams)
        kept, sent, *more = four_sections(step, index, edge, state, gathered, kernels, rim, maps, chosen)
        chosen = (kept, sent)
        if more:
            state, share = more
    other = lax.ppermute(sent, "segment", [(s, s ^ SPLIT) for s in range(8)])
    cotans = cotangent[0, :, 0].reshape(2, CELLS, C)
    mine = lax.dynamic_index_in_dim(cotans, sample, 0, False)
    theirs = lax.dynamic_index_in_dim(cotans, 1 - sample, 0, False)
    zero = jnp.zeros((TAPS * C, C), jnp.float32)
    level_mine, term = gradient(kept, mine, weights[0], zero, jnp.float32)
    level_other, term = gradient(other, theirs, weights[0], term, jnp.bfloat16)
    total = sum_terms(term)
    low = jnp.where(sample == 0, level_mine, level_other)
    high = jnp.where(sample == 0, level_other, level_mine)
    levels = jnp.stack([low, high]).reshape(1, 2, 1, SIDE, SIDE, C)
    return levels, total[None]


def solution(mesh):
    placed = (
        P("dp", "tile", None, None, None),
        P(),
        P(),
        P(),
        P("segment", None, None),
        P("segment", "dp", "tile", None, None, None),
    )
    return jax.shard_map(
        local,
        mesh=mesh,
        in_specs=placed,
        out_specs=(P("segment", "dp", "tile", None, None, None), P("segment", None, None)),
        check_vma=False,
    )
```

```python
import jax
import jax.numpy as jnp
from jax import lax
from jax.experimental import pallas as pl
from jax.experimental.pallas import tpu as pltpu
from jax.sharding import PartitionSpec as P

SIDE = 32
CELLS = SIDE * SIDE
RING = 4 * SIDE
C = 128
TAPS = 9
DEPTH = 4
SPLIT = 4
PART = SIDE // SPLIT
EDGE = DEPTH * PART
SHARE = 4 * EDGE
BLOCKS = [[(x, c) for x in range(DEPTH + 1 - j) for c in range(DEPTH - j)] for j in range(1, DEPTH)]
SLOTS = sum(len(block) for block in BLOCKS)
FANS = 8
PICK = SHARE + FANS * SLOTS
VMEM_BYTES = 48 * 1024 * 1024


def iota(shape, axis):
    return lax.broadcasted_iota(jnp.int32, shape, axis)


def onehot(target, columns):
    return (target[:, None] == iota((target.shape[0], columns), 1)).astype(jnp.bfloat16)


def lookup(seams, slot):
    hit = slot[..., None] == jnp.arange(seams.shape[0], dtype=jnp.int32)
    found = jnp.sum(jnp.where(hit, seams, 0), axis=-1)
    return found // 8, found // 2 % 4, found % 2


def rim_cell(edge, depth, place):
    last = SIDE - 1
    return jnp.where(
        edge == 0,
        depth * SIDE + place,
        jnp.where(
            edge == 1,
            place * SIDE + last - depth,
            jnp.where(edge == 2, (last - depth) * SIDE + place, place * SIDE + depth),
        ),
    )


def walk(seams, tile, edge, end):
    corner = jnp.where((edge == 0) | (edge == 3), 0, 1)
    tile, edge, flip = lookup(seams, tile * 4 + jnp.where(edge % 2 == 0, 3 - 2 * end, 2 * end))
    return tile, edge, jnp.where(flip == 1, 1 - corner, corner)


def spread(columns, counts):
    return jnp.concatenate(
        [jnp.broadcast_to(col[..., None], col.shape + (n,)) for col, n in zip(columns, counts)], axis=-1
    )


def static(values):
    row = jnp.zeros((len(values),), jnp.int32)
    for i, value in enumerate(values):
        row = jnp.where(jnp.arange(len(values), dtype=jnp.int32) == i, value, row)
    return row


def tap_columns(edges, ends, block_of, x, c):
    k = iota((TAPS, 1, 1), 0)
    dy, dx = k // 3 - 1, k % 3 - 1
    edges, ends = edges[None], ends[None]
    down = jnp.where(edges == 0, dy, jnp.where(edges == 2, -dy, jnp.where(edges == 3, dx, -dx)))
    along = jnp.where(edges % 2 == 0, dx, dy)
    along = jnp.where(ends == 1, -along, along)
    return x + along, c + down


def selections(neighbor, edge_of, reverse, tile, part, columns):
    seams = (neighbor * 8 + edge_of * 2 + reverse).reshape(-1)
    row = jnp.arange(SHARE, dtype=jnp.int32)
    share = rim_cell(row // EDGE, row // PART % DEPTH, part * PART + row % PART)
    rim = onehot(share, CELLS)
    targets = jnp.arange(neighbor.shape[0] // columns, dtype=jnp.int32)[:, None] * columns + tile % columns
    fan = jnp.arange(FANS, dtype=jnp.int32)
    nbr, edge, flip = lookup(seams, targets * 4 + fan // 2)
    chain = [(nbr, edge, jnp.broadcast_to(fan % 2, nbr.shape))]
    for j in range(1, DEPTH):
        chain.append(walk(seams, *chain[-1]))
    around, edges, ends = zip(*chain[1:])
    counts = [len(block) for block in BLOCKS]
    x = static([cell[0] for block in BLOCKS for cell in block])
    c = static([cell[1] for block in BLOCKS for cell in block])
    along = jnp.where(spread(ends, counts) == 1, SIDE - 1 - x, x)
    inner = spread(edges, counts) * EDGE + c * PART + along % PART
    inner = jnp.where(along // PART == part, inner, -SHARE * columns)
    strip = [nbr[:, 0::2], edge[:, 0::2]]
    strip = [jnp.concatenate([jnp.broadcast_to(v[:, d : d + 1], (v.shape[0], EDGE)) for d in range(4)], 1) for v in strip]
    source = jnp.concatenate([strip[0], spread(around, counts).reshape(-1, FANS * SLOTS)], axis=1)
    place = jnp.concatenate([strip[1] * EDGE + row % EDGE, inner.reshape(-1, FANS * SLOTS)], axis=1)
    place = jnp.where(source // columns == tile // columns, source % columns * SHARE + place, -1)
    pick = onehot(place.reshape(-1), columns * SHARE)
    mine = (targets == tile).astype(jnp.int32)
    edge, flip = jnp.sum(edge * mine, axis=0)[0::2], jnp.sum(flip * mine, axis=0)[0::2]
    edges = [jnp.sum(v * mine, axis=0) for v in edges]
    ends = [jnp.sum(v * mine, axis=0) for v in ends]
    d, place = row // SIDE, row % SIDE
    end = jnp.where(place == 0, 0, jnp.where(place == SIDE - 1, 1, -1))
    beyond = []
    for slots, stride, rows in ((SLOTS, 3, 4), (8, 2, 3), (2, 1, 2)):
        target = (d * 2 + end)[None] * slots + stride * jnp.arange(rows, dtype=jnp.int32)[:, None]
        target = jnp.where(end[None] < 0, -1, target)
        beyond.append(onehot(target.reshape(-1), FANS * slots))
    fan3 = iota((1, FANS, 1), 1)
    at_end = fan3 // 2 * SIDE + fan3 % 2 * (SIDE - 1)
    x = static([0, 0, 1, 1, 2, 2, 0, 1])
    c = static([0, 1, 0, 1, 0, 1, 0, 0])
    near = jnp.arange(8, dtype=jnp.int32) < 6
    x, c = tap_columns(spread(edges[:2], (6, 2)), spread(ends[:2], (6, 2)), near, x, c)
    base = DEPTH * RING + fan3 * SLOTS
    first = jnp.where(
        c < 0,
        jnp.where(near, x * RING + at_end, base + x),
        jnp.where(
            x < 0,
            jnp.where(near, base + 12 + 2 * c, base + 18 + c),
            jnp.where(near, base + 3 * x + c, base + 12 + 2 * x + c),
        ),
    )
    first = onehot(jnp.where((c < 0) & (x < 0), -1, first).reshape(-1), DEPTH * RING + FANS * SLOTS)
    x, c = tap_columns(spread(edges[:1], (2,)), spread(ends[:1], (2,)), None, static([0, 1]), static([0, 0]))
    base = (DEPTH - 1) * RING + fan3 * 8
    second = jnp.where(c < 0, x * RING + at_end, jnp.where(x < 0, base + 6 + c, base + 2 * x + c))
    second = onehot(jnp.where((c < 0) & (x < 0), -1, second).reshape(-1), (DEPTH - 1) * RING + FANS * 8)
    flip = jnp.concatenate([jnp.broadcast_to(flip[k : k + 1], (SIDE,)) for k in range(4)])
    turned = jnp.where(flip == 1, SIDE - 1 - place, place)
    facing = onehot(rim_cell(d, 0, turned), CELLS)
    turn = onehot(d * SIDE + turned, RING)
    return edge, rim, pick, (*beyond, first, second, facing, turn)


def sigmoid(value):
    return 1.0 / (1.0 + jnp.exp(-value))


def fill_patches(state, padded, patches):
    padded[1 : SIDE + 1, 8 : SIDE + 8, :] = (
        state[0:CELLS, :].astype(jnp.float32).reshape(SIDE, SIDE, C)
    )
    halo = state[CELLS : CELLS + RING, :].astype(jnp.float32)
    empty = jnp.zeros((8, C), jnp.float32)
    for row, first in ((0, 0), (SIDE + 1, 2 * SIDE)):
        padded[row, 0:8, :] = empty
        padded[row, 8 : SIDE + 8, :] = halo[first : first + SIDE]
        padded[row, SIDE + 8 : SIDE + 16, :] = empty
    padded[1 : SIDE + 1, SIDE + 8, :] = halo[SIDE : 2 * SIDE]
    padded[1 : SIDE + 1, 7, :] = halo[3 * SIDE : 4 * SIDE]
    for dx in range(3):
        shifted = padded[:, 7 + dx : 7 + dx + SIDE, :].astype(jnp.bfloat16)
        shifted = shifted.reshape((SIDE + 2) * SIDE, C)
        for dy in range(3):
            k = dy * 3 + dx
            patches[:, k * C : (k + 1) * C] = shifted[dy * SIDE : dy * SIDE + CELLS]


def next_state(state, pre_act):
    return (state + pre_act * sigmoid(pre_act)).astype(jnp.bfloat16)


def dot(a, b):
    return jnp.dot(a, b, preferred_element_type=jnp.float32)


def update_strips(edge, level, strips, ends, mine, weights, side_patches):
    rows = len(strips) - 1
    place = iota((RING, C), 0) % SIDE
    moved = []
    for cells, beyond in [(mine, jnp.zeros_like(mine))] + list(zip(strips, ends)):
        below = jnp.where(place == 0, beyond, pltpu.roll(cells, 1, 0))
        above = jnp.where(place == SIDE - 1, beyond, pltpu.roll(cells, RING - 1, 0))
        moved.append([v.astype(jnp.bfloat16) for v in (below, cells, above)])
    for d in range(4):
        e = edge[d]
        for a in range(3):
            across = jnp.where((e == 0) | (e == 3), a, 2 - a)
            for b in range(3):
                tap = jnp.where(e % 2 == 0, 3 * across + b, 3 * b + across)
                lanes = pl.ds(pl.multiple_of(tap * C, C), C)
                for r in range(rows):
                    first = r * RING + d * SIDE
                    side_patches[first : first + SIDE, lanes] = moved[r + a][b][d * SIDE : (d + 1) * SIDE]
    before = jnp.concatenate(strips[:rows], axis=0)
    after = next_state(before, dot(side_patches[0 : rows * RING, :], weights)).astype(jnp.float32)
    return [after[r * RING : (r + 1) * RING] for r in range(rows)]


def update_fans(taps, strips, fans, weights):
    pool = jnp.concatenate([v.astype(jnp.bfloat16) for v in strips + [fans]], axis=0)
    found = dot(taps[...], pool)
    n = found.shape[0] // TAPS
    parts = [found[k * n : (k + 1) * n] for k in range(TAPS)]
    side = jnp.concatenate([v.astype(jnp.bfloat16) for v in parts], axis=1)
    return next_state(parts[4], dot(side, weights)).astype(jnp.float32)


def round_kernel(step, last, *refs):
    index, edge, start, gathered, all_weights, rim, e0, e1, e2, taps1, taps2, facing, turn = refs[:13]
    refs = refs[13 + (2 if step else 0) :]
    (kept, sent), refs = refs[:2], refs[2:]
    if not last:
        (out, share), refs = refs[:2], refs[2:]
    states, padded, patches, side_patches, weights, weight_sems, sems = refs
    loads = [
        pltpu.make_async_copy(all_weights.at[step * DEPTH + i], weights.at[i], weight_sems.at[i])
        for i in range(DEPTH)
    ]
    for load in loads:
        load.start()
    states[0, 0:CELLS, :] = start[...]
    cells = gathered[...].astype(jnp.float32)
    strips = [
        jnp.concatenate(
            [
                cells[q * PICK + d * EDGE + r * PART : q * PICK + d * EDGE + (r + 1) * PART]
                for d in range(4)
                for q in range(SPLIT)
            ],
            axis=0,
        )
        for r in range(DEPTH)
    ]
    fans = cells[SHARE:PICK]
    for q in range(1, SPLIT):
        fans = fans + cells[q * PICK + SHARE : (q + 1) * PICK]

    def deliver(i, act):
        for slot, target in ((0, kept), (1, sent)):

            @pl.when(index[slot] == step * DEPTH + i)
            def _():
                act(pltpu.make_async_copy(states.at[i], target, sems.at[slot]))

    for i in range(DEPTH):
        state = states.at[i]
        state[CELLS : CELLS + RING, :] = dot(turn[...], strips[0].astype(jnp.bfloat16)).astype(jnp.bfloat16)
        deliver(i, lambda copy: copy.start())
        tile = state[0:CELLS, :]
        if not (last and i == DEPTH - 1):
            fill_patches(state, padded, patches)
        loads[i].wait()
        if i < DEPTH - 1:
            ends = dot((e0, e1, e2)[i][...], fans.astype(jnp.bfloat16))
            ends = [ends[r * RING : (r + 1) * RING] for r in range(DEPTH - i)]
            mine = dot(facing[...], tile)
            moved = update_strips(edge, i, strips, ends, mine, weights[i], side_patches)
            if i < DEPTH - 2:
                fans = update_fans((taps1, taps2)[i], strips, fans, weights[i])
            strips = moved
        if not (last and i == DEPTH - 1):
            new = next_state(tile.astype(jnp.float32), dot(patches[...], weights[i]))
            if i < DEPTH - 1:
                states[i + 1, 0:CELLS, :] = new
            else:
                out[...] = new
                share[...] = dot(rim[...], new).astype(jnp.bfloat16)
    for i in range(DEPTH):
        deliver(i, lambda copy: copy.wait())


def four_sections(step, index, edge, start, gathered, weights, rim, maps, chosen):
    last = step == 1
    vmem = pl.BlockSpec(memory_space=pltpu.VMEM)
    smem = pl.BlockSpec(memory_space=pltpu.SMEM)
    hbm = pl.BlockSpec(memory_space=pl.ANY)
    bf16 = jnp.bfloat16
    state = jax.ShapeDtypeStruct((CELLS + RING, C), bf16)
    outs = [state, state]
    if not last:
        outs += [jax.ShapeDtypeStruct((CELLS, C), bf16), jax.ShapeDtypeStruct((SHARE, C), bf16)]
    return pl.pallas_call(
        lambda *refs: round_kernel(step, last, *refs),
        out_shape=outs,
        in_specs=[smem] * 2 + [vmem] * 2 + [pl.BlockSpec(memory_space=pltpu.HBM)] + [vmem] * 8 + [hbm] * len(chosen),
        out_specs=[hbm] * 2 + [vmem] * (len(outs) - 2),
        scratch_shapes=[
            pltpu.VMEM((DEPTH, CELLS + RING, C), bf16),
            pltpu.VMEM((SIDE + 2, SIDE + 16, C), jnp.float32),
            pltpu.VMEM((CELLS, TAPS * C), bf16),
            pltpu.VMEM(((DEPTH - 1) * RING, TAPS * C), bf16),
            pltpu.VMEM((DEPTH, TAPS * C, C), bf16),
            pltpu.SemaphoreType.DMA((DEPTH,)),
            pltpu.SemaphoreType.DMA((2,)),
        ],
        input_output_aliases={13 + i: i for i in range(len(chosen))},
        compiler_params=pltpu.CompilerParams(vmem_limit_bytes=VMEM_BYTES),
        cost_estimate=pl.CostEstimate(
            flops=2 * DEPTH * CELLS * TAPS * C * C, bytes_accessed=6 << 20, transcendentals=DEPTH * CELLS * C
        ),
        name="four_sections",
    )(index, edge, start, gathered, weights, rim, *maps, *chosen)


def gradient_kernel(state, cotangent, weights, before, level, term, padded, patches):
    fill_patches(state, padded, patches)
    pre_act = dot(patches[...], weights[...])
    gate = sigmoid(pre_act)
    level[...] = (state[0:CELLS, :].astype(jnp.float32) + pre_act * gate).astype(jnp.bfloat16)
    slope = gate * (1.0 + pre_act * (1.0 - gate))
    delta = (cotangent[...].astype(jnp.float32) * slope).astype(jnp.bfloat16)
    added = lax.dot_general(
        patches[...], delta, (((0,), (0,)), ((), ())), preferred_element_type=jnp.float32
    )
    term[...] = (before[...] + added).astype(term.dtype)


def gradient(state, cotangent, weights, before, dtype):
    vmem = pl.BlockSpec(memory_space=pltpu.VMEM)
    return pl.pallas_call(
        gradient_kernel,
        out_shape=(
            jax.ShapeDtypeStruct((CELLS, C), jnp.bfloat16),
            jax.ShapeDtypeStruct((TAPS * C, C), dtype),
        ),
        in_specs=[vmem] * 4,
        out_specs=(vmem,) * 2,
        scratch_shapes=[
            pltpu.VMEM((SIDE + 2, SIDE + 16, C), jnp.float32),
            pltpu.VMEM((CELLS, TAPS * C), jnp.bfloat16),
        ],
        compiler_params=pltpu.CompilerParams(vmem_limit_bytes=VMEM_BYTES),
        cost_estimate=pl.CostEstimate(
            flops=2 * 2 * CELLS * TAPS * C * C, bytes_accessed=3 << 20, transcendentals=CELLS * C
        ),
        name="gradient",
    )(state, cotangent, weights, before)


def share_out(block, axis, groups=None):
    count = lax.axis_size(axis) if groups is None else len(groups[0])
    return lax.all_to_all(
        jnp.broadcast_to(block[None], (count,) + block.shape), axis, 0, 0, axis_index_groups=groups
    )


def sum_terms(term):
    count = lax.axis_size("tile")
    rows = term.shape[0] // count
    pieces = lax.all_to_all(term.reshape(count, rows, term.shape[1]), "tile", 0, 0)
    piece = jnp.sum(pieces.astype(jnp.float32), axis=0).astype(jnp.bfloat16)
    pieces = share_out(piece, ("dp", "tile")).reshape((lax.axis_size("dp"),) + term.shape)
    return jnp.sum(pieces.astype(jnp.float32), axis=0)


def local(inputs, neighbor, edge_of, reverse, weights, cotangent):
    segment = lax.axis_index("segment")
    sample, part = segment // SPLIT, segment % SPLIT
    partner = segment ^ SPLIT
    teams = [[t * SPLIT + p for p in range(SPLIT)] for t in range(2)]
    kernels = lax.all_gather(weights, "segment", axis=0, tiled=True)
    tiles = neighbor.shape[0]
    rows = 4 if tiles % 8 == 0 else 2
    columns = tiles // rows
    along_row = [[r * columns + c for c in range(columns)] for r in range(rows)]
    along_column = [[r * columns + c for r in range(rows)] for c in range(columns)]
    edge, rim, pick, maps = selections(neighbor, edge_of, reverse, lax.axis_index("tile"), part, columns)
    index = jnp.stack([segment, partner]).astype(jnp.int32)
    state = lax.dynamic_index_in_dim(inputs[:, 0], sample, 0, False).reshape(CELLS, C)
    share = dot(rim, state).astype(jnp.bfloat16)
    chosen = ()
    for step in range(2):
        rims = share_out(share, "tile", along_row).reshape(-1, C)
        picked = dot(pick, rims).astype(jnp.bfloat16).reshape(rows, PICK, C)
        picked = lax.all_to_all(picked, "tile", 0, 0, axis_index_groups=along_column)
        picked = jnp.sum(picked.astype(jnp.float32), axis=0).astype(jnp.bfloat16)
        gathered = lax.all_gather(picked, "segment", axis=0, tiled=True, axis_index_groups=teams)
        kept, sent, *more = four_sections(step, index, edge, state, gathered, kernels, rim, maps, chosen)
        chosen = (kept, sent)
        if more:
            state, share = more
    other = lax.ppermute(sent, "segment", [(s, s ^ SPLIT) for s in range(8)])
    cotans = cotangent[0, :, 0].reshape(2, CELLS, C)
    mine = lax.dynamic_index_in_dim(cotans, sample, 0, False)
    theirs = lax.dynamic_index_in_dim(cotans, 1 - sample, 0, False)
    zero = jnp.zeros((TAPS * C, C), jnp.float32)
    level_mine, term = gradient(kept, mine, weights[0], zero, jnp.float32)
    level_other, term = gradient(other, theirs, weights[0], term, jnp.bfloat16)
    total = sum_terms(term)
    low = jnp.where(sample == 0, level_mine, level_other)
    high = jnp.where(sample == 0, level_other, level_mine)
    levels = jnp.stack([low, high]).reshape(1, 2, 1, SIDE, SIDE, C)
    return levels, total[None]


def solution(mesh):
    placed = (
        P("dp", "tile", None, None, None),
        P(),
        P(),
        P(),
        P("segment", None, None),
        P("segment", "dp", "tile", None, None, None),
    )
    return jax.shard_map(
        local,
        mesh=mesh,
        in_specs=placed,
        out_specs=(P("segment", "dp", "tile", None, None, None), P("segment", None, None)),
        check_vma=False,
    )
```

```python
import jax
import jax.numpy as jnp
from jax import lax
from jax.experimental import pallas as pl
from jax.experimental.pallas import tpu as pltpu
from jax.sharding import PartitionSpec as P

SIDE = 32
CELLS = SIDE * SIDE
RING = 4 * SIDE
C = 128
TAPS = 9
DEPTH = 4
SPLIT = 4
PART = SIDE // SPLIT
EDGE = DEPTH * PART
STRIPS = 4 * EDGE
BLOCKS = [(1, 0), (1, 1), (1, 2), (2, 0), (2, 1), (3, 0)]
FANS = 8
SLOTS = len(BLOCKS)
SHARE = STRIPS + 32
PICK = STRIPS + FANS * SLOTS
AROUND = SPLIT * FANS * SLOTS
VMEM_BYTES = 20 * 1024 * 1024


def iota(shape, axis):
    return lax.broadcasted_iota(jnp.int32, shape, axis)


def onehot(target, columns):
    return (target[:, None] == iota((target.shape[0], columns), 1)).astype(jnp.bfloat16)


def lookup(seams, slot):
    hit = slot[..., None] == jnp.arange(seams.shape[0], dtype=jnp.int32)
    found = jnp.sum(jnp.where(hit, seams, 0), axis=-1)
    return found // 8, found // 2 % 4, found % 2


def rim_cell(edge, depth, place):
    last = SIDE - 1
    return jnp.where(
        edge == 0,
        depth * SIDE + place,
        jnp.where(
            edge == 1,
            place * SIDE + last - depth,
            jnp.where(edge == 2, (last - depth) * SIDE + place, place * SIDE + depth),
        ),
    )


def walk(seams, tile, edge, end):
    corner = jnp.where((edge == 0) | (edge == 3), 0, 1)
    tile, edge, flip = lookup(seams, tile * 4 + jnp.where(edge % 2 == 0, 3 - 2 * end, 2 * end))
    return tile, edge, jnp.where(flip == 1, 1 - corner, corner)


def spread(columns, counts):
    return jnp.concatenate(
        [jnp.broadcast_to(col[..., None], col.shape + (n,)) for col, n in zip(columns, counts)], axis=-1
    )


def static(values):
    row = jnp.zeros((len(values),), jnp.int32)
    for i, value in enumerate(values):
        row = jnp.where(jnp.arange(len(values), dtype=jnp.int32) == i, value, row)
    return row


def tap_columns(edges, ends, block_of, x, c):
    k = iota((TAPS, 1, 1), 0)
    dy, dx = k // 3 - 1, k % 3 - 1
    edges, ends = edges[None], ends[None]
    down = jnp.where(edges == 0, dy, jnp.where(edges == 2, -dy, jnp.where(edges == 3, dx, -dx)))
    along = jnp.where(edges % 2 == 0, dx, dy)
    along = jnp.where(ends == 1, -along, along)
    return x + along, c + down


def selections(neighbor, edge_of, reverse, tile, part, columns):
    seams = (neighbor * 8 + edge_of * 2 + reverse).reshape(-1)
    row = jnp.arange(STRIPS, dtype=jnp.int32)
    share = rim_cell(row // EDGE, row // PART % DEPTH, part * PART + row % PART)
    corner = jnp.arange(SHARE - STRIPS, dtype=jnp.int32)
    spot = rim_cell(corner // 6, corner % 3, jnp.where(corner // 3 % 2 == 1, SIDE - 1 - part, part))
    rim = onehot(jnp.concatenate([share, jnp.where(corner < 24, spot, -1)]), CELLS)
    targets = jnp.arange(neighbor.shape[0] // columns, dtype=jnp.int32)[:, None] * columns + tile % columns
    fan = jnp.arange(FANS, dtype=jnp.int32)
    nbr, edge, flip = lookup(seams, targets * 4 + fan // 2)
    chain = [(nbr, edge, jnp.broadcast_to(fan % 2, nbr.shape))]
    for j in range(1, DEPTH):
        chain.append(walk(seams, *chain[-1]))
    around, edges, ends = zip(*chain[1:])
    counts = [sum(1 for block in BLOCKS if block[0] == j) for j in range(1, DEPTH)]
    j = static([block[0] for block in BLOCKS])
    c = static([block[1] for block in BLOCKS])
    inner = STRIPS + (spread(edges, counts) * 2 + spread(ends, counts)) * 3 + c
    inner = jnp.where(part + j <= DEPTH, inner, -SHARE * columns)
    strip = [nbr[:, 0::2], edge[:, 0::2]]
    strip = [jnp.concatenate([jnp.broadcast_to(v[:, d : d + 1], (v.shape[0], EDGE)) for d in range(4)], 1) for v in strip]
    source = jnp.concatenate([strip[0], spread(around, counts).reshape(-1, FANS * SLOTS)], axis=1)
    place = jnp.concatenate([strip[1] * EDGE + row % EDGE, inner.reshape(-1, FANS * SLOTS)], axis=1)
    place = jnp.where(source // columns == tile // columns, source % columns * SHARE + place, -1)
    pick = onehot(place.reshape(-1), columns * SHARE)
    mine = (targets == tile).astype(jnp.int32)
    edge, flip = jnp.sum(edge * mine, axis=0)[0::2], jnp.sum(flip * mine, axis=0)[0::2]
    edges = [jnp.sum(v * mine, axis=0) for v in edges]
    ends = [jnp.sum(v * mine, axis=0) for v in ends]
    d, place = row // SIDE, row % SIDE
    end = jnp.where(place == 0, 0, jnp.where(place == SIDE - 1, 1, -1))
    beyond = []
    for slots, stride, rows, count in ((SLOTS, FANS * SLOTS, 4, AROUND), (8, 2, 3, 64), (2, 1, 2, 16)):
        target = (d * 2 + end)[None] * slots + stride * jnp.arange(rows, dtype=jnp.int32)[:, None]
        target = jnp.where(end[None] < 0, -1, target)
        beyond.append(onehot(target.reshape(-1), count))
    fan3 = iota((1, FANS, 1), 1)
    at_end = fan3 // 2 * SIDE + fan3 % 2 * (SIDE - 1)
    x = static([0, 0, 1, 1, 2, 2, 0, 1])
    c = static([0, 1, 0, 1, 0, 1, 0, 0])
    near = jnp.arange(8, dtype=jnp.int32) < 6
    x, c = tap_columns(spread(edges[:2], (6, 2)), spread(ends[:2], (6, 2)), near, x, c)
    base = DEPTH * RING + fan3 * SLOTS
    next_place = FANS * SLOTS
    first = jnp.where(
        c < 0,
        jnp.where(near, x * RING + at_end, base + x),
        jnp.where(
            x < 0,
            base + next_place * c + jnp.where(near, 3, 5),
            base + next_place * x + jnp.where(near, 0, 3) + c,
        ),
    )
    first = onehot(jnp.where((c < 0) & (x < 0), -1, first).reshape(-1), DEPTH * RING + AROUND)
    x, c = tap_columns(spread(edges[:1], (2,)), spread(ends[:1], (2,)), None, static([0, 1]), static([0, 0]))
    base = (DEPTH - 1) * RING + fan3 * 8
    second = jnp.where(c < 0, x * RING + at_end, jnp.where(x < 0, base + 6 + c, base + 2 * x + c))
    second = onehot(jnp.where((c < 0) & (x < 0), -1, second).reshape(-1), (DEPTH - 1) * RING + FANS * 8)
    flip = jnp.concatenate([jnp.broadcast_to(flip[k : k + 1], (SIDE,)) for k in range(4)])
    turned = jnp.where(flip == 1, SIDE - 1 - place, place)
    facing = onehot(rim_cell(d, 0, turned), CELLS)
    turn = onehot(d * SIDE + turned, RING)
    return edge, rim, pick, (*beyond, first, second, facing, turn)


def sigmoid(value):
    return 1.0 / (1.0 + jnp.exp(-value))


def fill_patches(state, padded, patches):
    padded[1 : SIDE + 1, 8 : SIDE + 8, :] = (
        state[0:CELLS, :].astype(jnp.float32).reshape(SIDE, SIDE, C)
    )
    halo = state[CELLS : CELLS + RING, :].astype(jnp.float32)
    empty = jnp.zeros((8, C), jnp.float32)
    for row, first in ((0, 0), (SIDE + 1, 2 * SIDE)):
        padded[row, 0:8, :] = empty
        padded[row, 8 : SIDE + 8, :] = halo[first : first + SIDE]
        padded[row, SIDE + 8 : SIDE + 16, :] = empty
    padded[1 : SIDE + 1, SIDE + 8, :] = halo[SIDE : 2 * SIDE]
    padded[1 : SIDE + 1, 7, :] = halo[3 * SIDE : 4 * SIDE]
    for dx in range(3):
        shifted = padded[:, 7 + dx : 7 + dx + SIDE, :].astype(jnp.bfloat16)
        shifted = shifted.reshape((SIDE + 2) * SIDE, C)
        for dy in range(3):
            k = dy * 3 + dx
            patches[:, k * C : (k + 1) * C] = shifted[dy * SIDE : dy * SIDE + CELLS]


def next_state(state, pre_act):
    return (state + pre_act * sigmoid(pre_act)).astype(jnp.bfloat16)


def dot(a, b):
    return jnp.dot(a, b, preferred_element_type=jnp.float32)


def update_strips(edge, level, strips, ends, mine, weights, side_patches):
    rows = len(strips) - 1
    place = iota((RING, C), 0) % SIDE
    moved = []
    for cells, beyond in [(mine, jnp.zeros_like(mine))] + list(zip(strips, ends)):
        below = jnp.where(place == 0, beyond, pltpu.roll(cells, 1, 0))
        above = jnp.where(place == SIDE - 1, beyond, pltpu.roll(cells, RING - 1, 0))
        moved.append([v.astype(jnp.bfloat16) for v in (below, cells, above)])
    for d in range(4):
        e = edge[d]
        for a in range(3):
            across = jnp.where((e == 0) | (e == 3), a, 2 - a)
            for b in range(3):
                tap = jnp.where(e % 2 == 0, 3 * across + b, 3 * b + across)
                lanes = pl.ds(pl.multiple_of(tap * C, C), C)
                for r in range(rows):
                    first = r * RING + d * SIDE
                    side_patches[first : first + SIDE, lanes] = moved[r + a][b][d * SIDE : (d + 1) * SIDE]
    before = jnp.concatenate(strips[:rows], axis=0)
    after = next_state(before, dot(side_patches[0 : rows * RING, :], weights)).astype(jnp.float32)
    return [after[r * RING : (r + 1) * RING] for r in range(rows)]


def update_fans(taps, strips, fans, weights):
    pool = jnp.concatenate([v.astype(jnp.bfloat16) for v in strips + [fans]], axis=0)
    found = dot(taps[...], pool)
    n = found.shape[0] // TAPS
    parts = [found[k * n : (k + 1) * n] for k in range(TAPS)]
    side = jnp.concatenate([v.astype(jnp.bfloat16) for v in parts], axis=1)
    return next_state(parts[4], dot(side, weights)).astype(jnp.float32)


def round_kernel(step, last, *refs):
    index, edge, start, gathered, all_weights, rim, e0, e1, e2, taps1, taps2, facing, turn = refs[:13]
    refs = refs[13 + (2 if step else 0) :]
    (kept, sent), refs = refs[:2], refs[2:]
    if not last:
        (out, share), refs = refs[:2], refs[2:]
    states, padded, patches, side_patches, weights, weight_sems, sems = refs
    loads = [
        pltpu.make_async_copy(all_weights.at[step * DEPTH + i], weights.at[i], weight_sems.at[i])
        for i in range(DEPTH)
    ]
    for load in loads:
        load.start()
    states[0, 0:CELLS, :] = start[...]
    cells = gathered[...].astype(jnp.float32)
    strips = [
        jnp.concatenate(
            [
                cells[q * PICK + d * EDGE + r * PART : q * PICK + d * EDGE + (r + 1) * PART]
                for d in range(4)
                for q in range(SPLIT)
            ],
            axis=0,
        )
        for r in range(DEPTH)
    ]
    fans = jnp.concatenate([cells[q * PICK + STRIPS : (q + 1) * PICK] for q in range(SPLIT)], axis=0)

    def deliver(i, act):
        for slot, target in ((0, kept), (1, sent)):

            @pl.when(index[slot] == step * DEPTH + i)
            def _():
                act(pltpu.make_async_copy(states.at[i], target, sems.at[slot]))

    for i in range(DEPTH):
        state = states.at[i]
        state[CELLS : CELLS + RING, :] = dot(turn[...], strips[0].astype(jnp.bfloat16)).astype(jnp.bfloat16)
        deliver(i, lambda copy: copy.start())
        tile = state[0:CELLS, :]
        if not (last and i == DEPTH - 1):
            fill_patches(state, padded, patches)
        loads[i].wait()
        if i < DEPTH - 1:
            ends = dot((e0, e1, e2)[i][...], fans.astype(jnp.bfloat16))
            ends = [ends[r * RING : (r + 1) * RING] for r in range(DEPTH - i)]
            mine = dot(facing[...], tile)
            moved = update_strips(edge, i, strips, ends, mine, weights[i], side_patches)
            if i < DEPTH - 2:
                fans = update_fans((taps1, taps2)[i], strips, fans, weights[i])
            strips = moved
        if not (last and i == DEPTH - 1):
            new = next_state(tile.astype(jnp.float32), dot(patches[...], weights[i]))
            if i < DEPTH - 1:
                states[i + 1, 0:CELLS, :] = new
            else:
                out[...] = new
                share[...] = dot(rim[...], new).astype(jnp.bfloat16)
    for i in range(DEPTH):
        deliver(i, lambda copy: copy.wait())


def four_sections(step, index, edge, start, gathered, weights, rim, maps, chosen):
    last = step == 1
    vmem = pl.BlockSpec(memory_space=pltpu.VMEM)
    smem = pl.BlockSpec(memory_space=pltpu.SMEM)
    hbm = pl.BlockSpec(memory_space=pl.ANY)
    bf16 = jnp.bfloat16
    state = jax.ShapeDtypeStruct((CELLS + RING, C), bf16)
    outs = [state, state]
    if not last:
        outs += [jax.ShapeDtypeStruct((CELLS, C), bf16), jax.ShapeDtypeStruct((SHARE, C), bf16)]
    return pl.pallas_call(
        lambda *refs: round_kernel(step, last, *refs),
        out_shape=outs,
        in_specs=[smem] * 2 + [vmem] * 2 + [pl.BlockSpec(memory_space=pltpu.HBM)] + [vmem] * 8 + [hbm] * len(chosen),
        out_specs=[hbm] * 2 + [vmem] * (len(outs) - 2),
        scratch_shapes=[
            pltpu.VMEM((DEPTH, CELLS + RING, C), bf16),
            pltpu.VMEM((SIDE + 2, SIDE + 16, C), jnp.float32),
            pltpu.VMEM((CELLS, TAPS * C), bf16),
            pltpu.VMEM(((DEPTH - 1) * RING, TAPS * C), bf16),
            pltpu.VMEM((DEPTH, TAPS * C, C), bf16),
            pltpu.SemaphoreType.DMA((DEPTH,)),
            pltpu.SemaphoreType.DMA((2,)),
        ],
        input_output_aliases={13 + i: i for i in range(len(chosen))},
        compiler_params=pltpu.CompilerParams(vmem_limit_bytes=VMEM_BYTES),
        cost_estimate=pl.CostEstimate(
            flops=2 * DEPTH * CELLS * TAPS * C * C, bytes_accessed=6 << 20, transcendentals=DEPTH * CELLS * C
        ),
        name="four_sections",
    )(index, edge, start, gathered, weights, rim, *maps, *chosen)


def gradient_kernel(last, state, cotangent, weights, before, level, term, padded, patches):
    fill_patches(state, padded, patches)
    pre_act = dot(patches[...], weights[...])
    gate = sigmoid(pre_act)
    level[...] = (state[0:CELLS, :].astype(jnp.float32) + pre_act * gate).astype(jnp.bfloat16)
    slope = gate * (1.0 + pre_act * (1.0 - gate))
    delta = (cotangent[...].astype(jnp.float32) * slope).astype(jnp.bfloat16)
    added = before[...] + lax.dot_general(
        delta, patches[...], (((0,), (0,)), ((), ())), preferred_element_type=jnp.float32
    )
    if not last:
        term[...] = added
        return
    for k in range(TAPS):
        term[k * C : (k + 1) * C, :] = added[:, k * C : (k + 1) * C].T.astype(jnp.bfloat16)


def gradient(state, cotangent, weights, before, last):
    vmem = pl.BlockSpec(memory_space=pltpu.VMEM)
    return pl.pallas_call(
        lambda *refs: gradient_kernel(last, *refs),
        out_shape=(
            jax.ShapeDtypeStruct((CELLS, C), jnp.bfloat16),
            jax.ShapeDtypeStruct((TAPS * C, C), jnp.bfloat16) if last else jax.ShapeDtypeStruct((C, TAPS * C), jnp.float32),
        ),
        in_specs=[vmem] * 4,
        out_specs=(vmem,) * 2,
        scratch_shapes=[
            pltpu.VMEM((SIDE + 2, SIDE + 16, C), jnp.float32),
            pltpu.VMEM((CELLS, TAPS * C), jnp.bfloat16),
        ],
        compiler_params=pltpu.CompilerParams(vmem_limit_bytes=VMEM_BYTES),
        cost_estimate=pl.CostEstimate(
            flops=2 * 2 * CELLS * TAPS * C * C, bytes_accessed=3 << 20, transcendentals=CELLS * C
        ),
        name="gradient",
    )(state, cotangent, weights, before)


def share_out(block, axis, groups=None):
    count = lax.axis_size(axis) if groups is None else len(groups[0])
    return lax.all_to_all(
        jnp.broadcast_to(block[None], (count,) + block.shape), axis, 0, 0, axis_index_groups=groups
    )


def sum_terms(term):
    count = lax.axis_size("tile")
    rows = term.shape[0] // count
    pieces = lax.all_to_all(term.reshape(count, rows, term.shape[1]), "tile", 0, 0)
    piece = jnp.sum(pieces.astype(jnp.float32), axis=0).astype(jnp.bfloat16)
    pieces = share_out(piece, ("dp", "tile")).reshape((lax.axis_size("dp"),) + term.shape)
    return jnp.sum(pieces.astype(jnp.float32), axis=0)


def local(inputs, neighbor, edge_of, reverse, weights, cotangent):
    segment = lax.axis_index("segment")
    sample, part = segment // SPLIT, segment % SPLIT
    partner = segment ^ SPLIT
    teams = [[t * SPLIT + p for p in range(SPLIT)] for t in range(2)]
    kernels = lax.all_gather(weights, "segment", axis=0, tiled=True)
    tiles = neighbor.shape[0]
    rows = 4 if tiles % 8 == 0 else 2
    columns = tiles // rows
    along_row = [[r * columns + c for c in range(columns)] for r in range(rows)]
    along_column = [[r * columns + c for r in range(rows)] for c in range(columns)]
    edge, rim, pick, maps = selections(neighbor, edge_of, reverse, lax.axis_index("tile"), part, columns)
    index = jnp.stack([segment, partner]).astype(jnp.int32)
    state = lax.dynamic_index_in_dim(inputs[:, 0], sample, 0, False).reshape(CELLS, C)
    share = dot(rim, state).astype(jnp.bfloat16)
    chosen = ()
    for step in range(2):
        rims = share_out(share, "tile", along_row).reshape(-1, C)
        picked = dot(pick, rims).astype(jnp.bfloat16).reshape(rows, PICK, C)
        picked = lax.all_to_all(picked, "tile", 0, 0, axis_index_groups=along_column)
        picked = jnp.sum(picked.astype(jnp.float32), axis=0).astype(jnp.bfloat16)
        gathered = lax.all_gather(picked, "segment", axis=0, tiled=True, axis_index_groups=teams)
        kept, sent, *more = four_sections(step, index, edge, state, gathered, kernels, rim, maps, chosen)
        chosen = (kept, sent)
        if more:
            state, share = more
    other = lax.ppermute(sent, "segment", [(s, s ^ SPLIT) for s in range(8)])
    cotans = cotangent[0, :, 0].reshape(2, CELLS, C)
    mine = lax.dynamic_index_in_dim(cotans, sample, 0, False)
    theirs = lax.dynamic_index_in_dim(cotans, 1 - sample, 0, False)
    zero = jnp.zeros((C, TAPS * C), jnp.float32)
    level_mine, term = gradient(kept, mine, weights[0], zero, False)
    level_other, term = gradient(other, theirs, weights[0], term, True)
    total = sum_terms(term)
    low = jnp.where(sample == 0, level_mine, level_other)
    high = jnp.where(sample == 0, level_other, level_mine)
    levels = jnp.stack([low, high]).reshape(1, 2, 1, SIDE, SIDE, C)
    return levels, total[None]


def solution(mesh):
    placed = (
        P("dp", "tile", None, None, None),
        P(),
        P(),
        P(),
        P("segment", None, None),
        P("segment", "dp", "tile", None, None, None),
    )
    return jax.shard_map(
        local,
        mesh=mesh,
        in_specs=placed,
        out_specs=(P("segment", "dp", "tile", None, None, None), P("segment", None, None)),
        check_vma=False,
    )
```

```python
import jax
import jax.numpy as jnp
from jax import lax
from jax.experimental import pallas as pl
from jax.experimental.pallas import tpu as pltpu
from jax.sharding import PartitionSpec as P

SIDE = 32
CELLS = SIDE * SIDE
RING = 4 * SIDE
C = 128
TAPS = 9
DEPTH = 4
SPLIT = 4
PART = SIDE // SPLIT
EDGE = DEPTH * PART
STRIPS = 4 * EDGE
BLOCKS = [(1, 0), (1, 1), (1, 2), (2, 0), (2, 1), (3, 0)]
FANS = 8
SLOTS = len(BLOCKS)
SHARE = STRIPS + 32
PICK = STRIPS + FANS * SLOTS
AROUND = SPLIT * FANS * SLOTS
VMEM_BYTES = 20 * 1024 * 1024


def iota(shape, axis):
    return lax.broadcasted_iota(jnp.int32, shape, axis)


def onehot(target, columns):
    return (target[:, None] == iota((target.shape[0], columns), 1)).astype(jnp.bfloat16)


def lookup(seams, slot):
    hit = slot[..., None] == jnp.arange(seams.shape[0], dtype=jnp.int32)
    found = jnp.sum(jnp.where(hit, seams, 0), axis=-1)
    return found // 8, found // 2 % 4, found % 2


def rim_cell(edge, depth, place):
    last = SIDE - 1
    return jnp.where(
        edge == 0,
        depth * SIDE + place,
        jnp.where(
            edge == 1,
            place * SIDE + last - depth,
            jnp.where(edge == 2, (last - depth) * SIDE + place, place * SIDE + depth),
        ),
    )


def walk(seams, tile, edge, end):
    corner = jnp.where((edge == 0) | (edge == 3), 0, 1)
    tile, edge, flip = lookup(seams, tile * 4 + jnp.where(edge % 2 == 0, 3 - 2 * end, 2 * end))
    return tile, edge, jnp.where(flip == 1, 1 - corner, corner)


def spread(columns, counts):
    return jnp.concatenate(
        [jnp.broadcast_to(col[..., None], col.shape + (n,)) for col, n in zip(columns, counts)], axis=-1
    )


def static(values):
    row = jnp.zeros((len(values),), jnp.int32)
    for i, value in enumerate(values):
        row = jnp.where(jnp.arange(len(values), dtype=jnp.int32) == i, value, row)
    return row


def tap_columns(edges, ends, block_of, x, c):
    k = iota((TAPS, 1, 1), 0)
    dy, dx = k // 3 - 1, k % 3 - 1
    edges, ends = edges[None], ends[None]
    down = jnp.where(edges == 0, dy, jnp.where(edges == 2, -dy, jnp.where(edges == 3, dx, -dx)))
    along = jnp.where(edges % 2 == 0, dx, dy)
    along = jnp.where(ends == 1, -along, along)
    return x + along, c + down


def selections(neighbor, edge_of, reverse, tile, part, columns):
    seams = (neighbor * 8 + edge_of * 2 + reverse).reshape(-1)
    row = jnp.arange(STRIPS, dtype=jnp.int32)
    share = rim_cell(row // EDGE, row // PART % DEPTH, part * PART + row % PART)
    corner = jnp.arange(SHARE - STRIPS, dtype=jnp.int32)
    spot = rim_cell(corner // 6, corner % 3, jnp.where(corner // 3 % 2 == 1, SIDE - 1 - part, part))
    rim = onehot(jnp.concatenate([share, jnp.where(corner < 24, spot, -1)]), CELLS)
    targets = jnp.arange(neighbor.shape[0] // columns, dtype=jnp.int32)[:, None] * columns + tile % columns
    fan = jnp.arange(FANS, dtype=jnp.int32)
    nbr, edge, flip = lookup(seams, targets * 4 + fan // 2)
    chain = [(nbr, edge, jnp.broadcast_to(fan % 2, nbr.shape))]
    for j in range(1, DEPTH):
        chain.append(walk(seams, *chain[-1]))
    around, edges, ends = zip(*chain[1:])
    counts = [sum(1 for block in BLOCKS if block[0] == j) for j in range(1, DEPTH)]
    j = static([block[0] for block in BLOCKS])
    c = static([block[1] for block in BLOCKS])
    inner = STRIPS + (spread(edges, counts) * 2 + spread(ends, counts)) * 3 + c
    inner = jnp.where(part + j <= DEPTH, inner, -SHARE * columns)
    strip = [nbr[:, 0::2], edge[:, 0::2]]
    strip = [jnp.concatenate([jnp.broadcast_to(v[:, d : d + 1], (v.shape[0], EDGE)) for d in range(4)], 1) for v in strip]
    source = jnp.concatenate([strip[0], spread(around, counts).reshape(-1, FANS * SLOTS)], axis=1)
    place = jnp.concatenate([strip[1] * EDGE + row % EDGE, inner.reshape(-1, FANS * SLOTS)], axis=1)
    place = jnp.where(source // columns == tile // columns, source % columns * SHARE + place, -1)
    pick = onehot(place.reshape(-1), columns * SHARE)
    mine = (targets == tile).astype(jnp.int32)
    edge, flip = jnp.sum(edge * mine, axis=0)[0::2], jnp.sum(flip * mine, axis=0)[0::2]
    edges = [jnp.sum(v * mine, axis=0) for v in edges]
    ends = [jnp.sum(v * mine, axis=0) for v in ends]
    d, place = row // SIDE, row % SIDE
    end = jnp.where(place == 0, 0, jnp.where(place == SIDE - 1, 1, -1))
    beyond = []
    for slots, stride, rows, count in ((SLOTS, FANS * SLOTS, 4, AROUND), (8, 2, 3, 64), (2, 1, 2, 16)):
        target = (d * 2 + end)[None] * slots + stride * jnp.arange(rows, dtype=jnp.int32)[:, None]
        target = jnp.where(end[None] < 0, -1, target)
        beyond.append(onehot(target.reshape(-1), count))
    fan3 = iota((1, FANS, 1), 1)
    at_end = fan3 // 2 * SIDE + fan3 % 2 * (SIDE - 1)
    x = static([0, 0, 1, 1, 2, 2, 0, 1])
    c = static([0, 1, 0, 1, 0, 1, 0, 0])
    near = jnp.arange(8, dtype=jnp.int32) < 6
    x, c = tap_columns(spread(edges[:2], (6, 2)), spread(ends[:2], (6, 2)), near, x, c)
    base = DEPTH * RING + fan3 * SLOTS
    next_place = FANS * SLOTS
    first = jnp.where(
        c < 0,
        jnp.where(near, x * RING + at_end, base + x),
        jnp.where(
            x < 0,
            base + next_place * c + jnp.where(near, 3, 5),
            base + next_place * x + jnp.where(near, 0, 3) + c,
        ),
    )
    first = onehot(jnp.where((c < 0) & (x < 0), -1, first).reshape(-1), DEPTH * RING + AROUND)
    x, c = tap_columns(spread(edges[:1], (2,)), spread(ends[:1], (2,)), None, static([0, 1]), static([0, 0]))
    base = (DEPTH - 1) * RING + fan3 * 8
    second = jnp.where(c < 0, x * RING + at_end, jnp.where(x < 0, base + 6 + c, base + 2 * x + c))
    second = onehot(jnp.where((c < 0) & (x < 0), -1, second).reshape(-1), (DEPTH - 1) * RING + FANS * 8)
    flip = jnp.concatenate([jnp.broadcast_to(flip[k : k + 1], (SIDE,)) for k in range(4)])
    turned = jnp.where(flip == 1, SIDE - 1 - place, place)
    facing = onehot(rim_cell(d, 0, turned), CELLS)
    turn = onehot(d * SIDE + turned, RING)
    return edge, rim, pick, (*beyond, first, second, facing, turn)


def sigmoid(value):
    return 1.0 / (1.0 + jnp.exp(-value))


def fill_patches(state, padded, patches):
    padded[1 : SIDE + 1, 8 : SIDE + 8, :] = (
        state[0:CELLS, :].astype(jnp.float32).reshape(SIDE, SIDE, C)
    )
    halo = state[CELLS : CELLS + RING, :].astype(jnp.float32)
    empty = jnp.zeros((8, C), jnp.float32)
    for row, first in ((0, 0), (SIDE + 1, 2 * SIDE)):
        padded[row, 0:8, :] = empty
        padded[row, 8 : SIDE + 8, :] = halo[first : first + SIDE]
        padded[row, SIDE + 8 : SIDE + 16, :] = empty
    padded[1 : SIDE + 1, SIDE + 8, :] = halo[SIDE : 2 * SIDE]
    padded[1 : SIDE + 1, 7, :] = halo[3 * SIDE : 4 * SIDE]
    for dx in range(3):
        shifted = padded[:, 7 + dx : 7 + dx + SIDE, :].astype(jnp.bfloat16)
        shifted = shifted.reshape((SIDE + 2) * SIDE, C)
        for dy in range(3):
            k = dy * 3 + dx
            patches[:, k * C : (k + 1) * C] = shifted[dy * SIDE : dy * SIDE + CELLS]


def next_state(state, pre_act):
    return (state + pre_act * sigmoid(pre_act)).astype(jnp.bfloat16)


def dot(a, b):
    return jnp.dot(a, b, preferred_element_type=jnp.float32)


def update_strips(edge, level, strips, ends, mine, weights, side_patches):
    rows = len(strips) - 1
    place = iota((RING, C), 0) % SIDE
    moved = []
    for cells, beyond in [(mine, jnp.zeros_like(mine))] + list(zip(strips, ends)):
        below = jnp.where(place == 0, beyond, pltpu.roll(cells, 1, 0))
        above = jnp.where(place == SIDE - 1, beyond, pltpu.roll(cells, RING - 1, 0))
        moved.append([v.astype(jnp.bfloat16) for v in (below, cells, above)])
    for d in range(4):
        e = edge[d]
        for a in range(3):
            across = jnp.where((e == 0) | (e == 3), a, 2 - a)
            for b in range(3):
                tap = jnp.where(e % 2 == 0, 3 * across + b, 3 * b + across)
                lanes = pl.ds(pl.multiple_of(tap * C, C), C)
                for r in range(rows):
                    first = r * RING + d * SIDE
                    side_patches[first : first + SIDE, lanes] = moved[r + a][b][d * SIDE : (d + 1) * SIDE]
    before = jnp.concatenate(strips[:rows], axis=0)
    after = next_state(before, dot(side_patches[0 : rows * RING, :], weights)).astype(jnp.float32)
    return [after[r * RING : (r + 1) * RING] for r in range(rows)]


def update_fans(taps, strips, fans, weights):
    pool = jnp.concatenate([v.astype(jnp.bfloat16) for v in strips + [fans]], axis=0)
    found = dot(taps[...], pool)
    n = found.shape[0] // TAPS
    parts = [found[k * n : (k + 1) * n] for k in range(TAPS)]
    side = jnp.concatenate([v.astype(jnp.bfloat16) for v in parts], axis=1)
    return next_state(parts[4], dot(side, weights)).astype(jnp.float32)


def round_kernel(step, last, *refs):
    index, edge, start, gathered, all_weights, rim, e0, e1, e2, taps1, taps2, facing, turn = refs[:13]
    refs = refs[13 + (2 if step else 0) :]
    (kept, sent), refs = refs[:2], refs[2:]
    if not last:
        (out, share), refs = refs[:2], refs[2:]
    states, padded, patches, side_patches, weights, weight_sems, sems = refs
    loads = [
        pltpu.make_async_copy(all_weights.at[step * DEPTH + i], weights.at[i], weight_sems.at[i])
        for i in range(DEPTH)
    ]
    for load in loads:
        load.start()
    states[0, 0:CELLS, :] = start[...]
    cells = gathered[...].astype(jnp.float32)
    strips = [
        jnp.concatenate(
            [
                cells[q * PICK + d * EDGE + r * PART : q * PICK + d * EDGE + (r + 1) * PART]
                for d in range(4)
                for q in range(SPLIT)
            ],
            axis=0,
        )
        for r in range(DEPTH)
    ]
    fans = jnp.concatenate([cells[q * PICK + STRIPS : (q + 1) * PICK] for q in range(SPLIT)], axis=0)

    def deliver(i, act):
        for slot, target in ((0, kept), (1, sent)):

            @pl.when(index[slot] == step * DEPTH + i)
            def _():
                act(pltpu.make_async_copy(states.at[i], target, sems.at[slot]))

    for i in range(DEPTH):
        state = states.at[i]
        state[CELLS : CELLS + RING, :] = dot(turn[...], strips[0].astype(jnp.bfloat16)).astype(jnp.bfloat16)
        deliver(i, lambda copy: copy.start())
        tile = state[0:CELLS, :]
        if not (last and i == DEPTH - 1):
            fill_patches(state, padded, patches)
        loads[i].wait()
        if i < DEPTH - 1:
            ends = dot((e0, e1, e2)[i][...], fans.astype(jnp.bfloat16))
            ends = [ends[r * RING : (r + 1) * RING] for r in range(DEPTH - i)]
            mine = dot(facing[...], tile)
            moved = update_strips(edge, i, strips, ends, mine, weights[i], side_patches)
            if i < DEPTH - 2:
                fans = update_fans((taps1, taps2)[i], strips, fans, weights[i])
            strips = moved
        if not (last and i == DEPTH - 1):
            new = next_state(tile.astype(jnp.float32), dot(patches[...], weights[i]))
            if i < DEPTH - 1:
                states[i + 1, 0:CELLS, :] = new
            else:
                out[...] = new
                share[...] = dot(rim[...], new).astype(jnp.bfloat16)
    for i in range(DEPTH):
        deliver(i, lambda copy: copy.wait())


def four_sections(step, index, edge, start, gathered, weights, rim, maps, chosen):
    last = step == 1
    vmem = pl.BlockSpec(memory_space=pltpu.VMEM)
    smem = pl.BlockSpec(memory_space=pltpu.SMEM)
    hbm = pl.BlockSpec(memory_space=pl.ANY)
    bf16 = jnp.bfloat16
    state = jax.ShapeDtypeStruct((CELLS + RING, C), bf16)
    outs = [state, state]
    if not last:
        outs += [jax.ShapeDtypeStruct((CELLS, C), bf16), jax.ShapeDtypeStruct((SHARE, C), bf16)]
    return pl.pallas_call(
        lambda *refs: round_kernel(step, last, *refs),
        out_shape=outs,
        in_specs=[smem] * 2 + [vmem] * 2 + [pl.BlockSpec(memory_space=pltpu.HBM)] + [vmem] * 8 + [hbm] * len(chosen),
        out_specs=[hbm] * 2 + [vmem] * (len(outs) - 2),
        scratch_shapes=[
            pltpu.VMEM((DEPTH, CELLS + RING, C), bf16),
            pltpu.VMEM((SIDE + 2, SIDE + 16, C), jnp.float32),
            pltpu.VMEM((CELLS, TAPS * C), bf16),
            pltpu.VMEM(((DEPTH - 1) * RING, TAPS * C), bf16),
            pltpu.VMEM((DEPTH, TAPS * C, C), bf16),
            pltpu.SemaphoreType.DMA((DEPTH,)),
            pltpu.SemaphoreType.DMA((2,)),
        ],
        input_output_aliases={13 + i: i for i in range(len(chosen))},
        compiler_params=pltpu.CompilerParams(vmem_limit_bytes=VMEM_BYTES),
        cost_estimate=pl.CostEstimate(
            flops=2 * DEPTH * CELLS * TAPS * C * C, bytes_accessed=6 << 20, transcendentals=DEPTH * CELLS * C
        ),
        name="four_sections",
    )(index, edge, start, gathered, weights, rim, *maps, *chosen)


def gradient_kernel(last, index, state, cotangents, weights, before, level, term, padded, patches, cotangent, sem):
    load = pltpu.make_async_copy(cotangents.at[index[0]], cotangent, sem)
    load.start()
    fill_patches(state, padded, patches)
    pre_act = dot(patches[...], weights[...])
    load.wait()
    gate = sigmoid(pre_act)
    level[...] = (state[0:CELLS, :].astype(jnp.float32) + pre_act * gate).astype(jnp.bfloat16)
    slope = gate * (1.0 + pre_act * (1.0 - gate))
    delta = (cotangent[...].astype(jnp.float32) * slope).astype(jnp.bfloat16)
    added = before[...] + lax.dot_general(
        delta, patches[...], (((0,), (0,)), ((), ())), preferred_element_type=jnp.float32
    )
    if not last:
        term[...] = added
        return
    for k in range(TAPS):
        term[k * C : (k + 1) * C, :] = added[:, k * C : (k + 1) * C].T.astype(jnp.bfloat16)


def gradient(sample, state, cotangents, weights, before, last):
    vmem = pl.BlockSpec(memory_space=pltpu.VMEM)
    smem = pl.BlockSpec(memory_space=pltpu.SMEM)
    hbm = pl.BlockSpec(memory_space=pltpu.HBM)
    return pl.pallas_call(
        lambda *refs: gradient_kernel(last, *refs),
        out_shape=(
            jax.ShapeDtypeStruct((CELLS, C), jnp.bfloat16),
            jax.ShapeDtypeStruct((TAPS * C, C), jnp.bfloat16) if last else jax.ShapeDtypeStruct((C, TAPS * C), jnp.float32),
        ),
        in_specs=[smem, vmem, hbm, vmem, vmem],
        out_specs=(vmem,) * 2,
        scratch_shapes=[
            pltpu.VMEM((SIDE + 2, SIDE + 16, C), jnp.float32),
            pltpu.VMEM((CELLS, TAPS * C), jnp.bfloat16),
            pltpu.VMEM((CELLS, C), jnp.bfloat16),
            pltpu.SemaphoreType.DMA,
        ],
        compiler_params=pltpu.CompilerParams(vmem_limit_bytes=VMEM_BYTES),
        cost_estimate=pl.CostEstimate(
            flops=2 * 2 * CELLS * TAPS * C * C, bytes_accessed=3 << 20, transcendentals=CELLS * C
        ),
        name="gradient",
    )(sample, state, cotangents, weights, before)


def add_parts_kernel(parts, out):
    total = parts[0].astype(jnp.float32)
    for i in range(1, parts.shape[0]):
        total = total + parts[i].astype(jnp.float32)
    out[...] = total.astype(out.dtype)


def add_parts(parts):
    vmem = pl.BlockSpec(memory_space=pltpu.VMEM)
    return pl.pallas_call(
        add_parts_kernel,
        out_shape=jax.ShapeDtypeStruct(parts.shape[1:], parts.dtype),
        in_specs=[vmem],
        out_specs=vmem,
        compiler_params=pltpu.CompilerParams(vmem_limit_bytes=4 * 1024 * 1024),
        cost_estimate=pl.CostEstimate(flops=parts.size, bytes_accessed=4 * parts.size, transcendentals=0),
        name="add_parts",
    )(parts)


def share_out(block, axis, groups=None):
    count = lax.axis_size(axis) if groups is None else len(groups[0])
    return lax.all_to_all(
        jnp.broadcast_to(block[None], (count,) + block.shape), axis, 0, 0, axis_index_groups=groups
    )


def sum_terms(term):
    count = lax.axis_size("tile")
    rows = term.shape[0] // count
    pieces = lax.all_to_all(term.reshape(count, rows, term.shape[1]), "tile", 0, 0)
    piece = jnp.sum(pieces.astype(jnp.float32), axis=0).astype(jnp.bfloat16)
    pieces = share_out(piece, ("dp", "tile")).reshape((lax.axis_size("dp"),) + term.shape)
    return jnp.sum(pieces.astype(jnp.float32), axis=0)


def local(inputs, neighbor, edge_of, reverse, weights, cotangent):
    segment = lax.axis_index("segment")
    sample, part = segment // SPLIT, segment % SPLIT
    partner = segment ^ SPLIT
    teams = [[t * SPLIT + p for p in range(SPLIT)] for t in range(2)]
    kernels = lax.all_gather(weights, "segment", axis=0, tiled=True)
    tiles = neighbor.shape[0]
    rows = 4 if tiles % 8 == 0 else 2
    columns = tiles // rows
    along_row = [[r * columns + c for c in range(columns)] for r in range(rows)]
    along_column = [[r * columns + c for r in range(rows)] for c in range(columns)]
    edge, rim, pick, maps = selections(neighbor, edge_of, reverse, lax.axis_index("tile"), part, columns)
    index = jnp.stack([segment, partner]).astype(jnp.int32)
    state = lax.dynamic_index_in_dim(inputs[:, 0], sample, 0, False).reshape(CELLS, C)
    share = dot(rim, state).astype(jnp.bfloat16)
    chosen = ()
    for step in range(2):
        rims = share_out(share, "tile", along_row).reshape(-1, C)
        picked = dot(pick, rims).astype(jnp.bfloat16).reshape(rows, PICK, C)
        picked = lax.all_to_all(picked, "tile", 0, 0, axis_index_groups=along_column)
        picked = add_parts(picked)
        gathered = lax.all_gather(picked, "segment", axis=0, tiled=True, axis_index_groups=teams)
        kept, sent, *more = four_sections(step, index, edge, state, gathered, kernels, rim, maps, chosen)
        chosen = (kept, sent)
        if more:
            state, share = more
    other = lax.ppermute(sent, "segment", [(s, s ^ SPLIT) for s in range(8)])
    cotans = cotangent[0, :, 0].reshape(2, CELLS, C)
    mine, theirs = sample.reshape(1).astype(jnp.int32), (1 - sample).reshape(1).astype(jnp.int32)
    zero = jnp.zeros((C, TAPS * C), jnp.float32)
    level_mine, term = gradient(mine, kept, cotans, weights[0], zero, False)
    level_other, term = gradient(theirs, other, cotans, weights[0], term, True)
    total = sum_terms(term)
    low = jnp.where(sample == 0, level_mine, level_other)
    high = jnp.where(sample == 0, level_other, level_mine)
    levels = jnp.stack([low, high]).reshape(1, 2, 1, SIDE, SIDE, C)
    return levels, total[None]


def solution(mesh):
    placed = (
        P("dp", "tile", None, None, None),
        P(),
        P(),
        P(),
        P("segment", None, None),
        P("segment", "dp", "tile", None, None, None),
    )
    return jax.shard_map(
        local,
        mesh=mesh,
        in_specs=placed,
        out_specs=(P("segment", "dp", "tile", None, None, None), P("segment", None, None)),
        check_vma=False,
    )
```

```python
import jax
import jax.numpy as jnp
import numpy as np
from jax import lax
from jax.experimental import pallas as pl
from jax.experimental.pallas import tpu as pltpu
from jax.sharding import PartitionSpec as P

SIDE = 32
CELLS = SIDE * SIDE
RING = 4 * SIDE
C = 128
TAPS = 9
DEPTH = 8
SPLIT = 4
PART = SIDE // SPLIT
EDGE = DEPTH * PART
SHARE = 4 * EDGE
FANS = 8
VMEM_BYTES = 26 * 1024 * 1024


def round_up(value, step):
    return -(-value // step) * step


def block_cells(depth):
    return [
        (j, c, x) for j in range(1, depth) for c in range(depth - j) for x in range(depth - j + 1)
    ]


SLOTS = [(j, c, x) for j in range(1, DEPTH) for c in range(DEPTH - j) for x in range((DEPTH - j) // SPLIT + 1)]
SLOT_ROWS = round_up(len(SLOTS), 8)
PICK = SHARE + FANS * SLOT_ROWS
FAN_ROWS = round_up(len(block_cells(DEPTH)) + 8, 16)


def iota(shape, axis):
    return lax.broadcasted_iota(jnp.int32, shape, axis)


def onehot(target, columns):
    return (target[:, None] == iota((target.shape[0], columns), 1)).astype(jnp.bfloat16)


def lookup(seams, slot):
    hit = slot[..., None] == jnp.arange(seams.shape[0], dtype=jnp.int32)
    found = jnp.sum(jnp.where(hit, seams, 0), axis=-1)
    return found // 8, found // 2 % 4, found % 2


def rim_cell(edge, depth, place):
    last = SIDE - 1
    return jnp.where(
        edge == 0,
        depth * SIDE + place,
        jnp.where(
            edge == 1,
            place * SIDE + last - depth,
            jnp.where(edge == 2, (last - depth) * SIDE + place, place * SIDE + depth),
        ),
    )


def walk(seams, tile, edge, end):
    corner = jnp.where((edge == 0) | (edge == 3), 0, 1)
    tile, edge, flip = lookup(seams, tile * 4 + jnp.where(edge % 2 == 0, 3 - 2 * end, 2 * end))
    return tile, edge, jnp.where(flip == 1, 1 - corner, corner)


def spread(columns, steps):
    picked = [columns[max(j, 1) - 1] for j in steps]
    return jnp.stack(picked, axis=-1)


def pad_cells(cells, count):
    cells = cells + [(0, 0, 0)] * (count - len(cells))
    return [np.array(column, np.int32) for column in zip(*cells)]


def fan_taps(depth, edges, ends):
    cells, targets = block_cells(depth), block_cells(depth - 1)
    rows = round_up(len(targets), 16)
    after = round_up(len(cells), 8)
    j, c, x = pad_cells(targets, rows)
    k = iota((1, TAPS, 1), 1)
    dy, dx = k // 3 - 1, k % 3 - 1
    edge, end = spread(edges, j)[:, None], spread(ends, j)[:, None]
    down = jnp.where(edge == 0, dy, jnp.where(edge == 2, -dy, jnp.where(edge == 3, dx, -dx)))
    along = jnp.where(edge % 2 == 0, dx, dy)
    along = jnp.where(end == 1, -along, along)
    x, c = x + along, c + down
    first = np.array([sum(1 for cell in cells if cell[0] < step) for step in range(depth + 1)], np.int32)
    width = depth + 1 - np.arange(depth + 1, dtype=np.int32)
    inside = first[j] + c * width[j] + x
    before = jnp.where(j == 1, after + x, first[np.maximum(j - 1, 0)] + x * width[np.maximum(j - 1, 0)])
    beyond = first[np.minimum(j + 1, depth)] + c
    column = jnp.where(c < 0, jnp.where(x < 0, -1, before), jnp.where(x < 0, beyond, inside))
    column = jnp.where(j == 0, -1, column)
    return onehot(column.reshape(-1), round_up(after + 8, 16))


def selections(neighbor, edge_of, reverse, tile, part, columns):
    seams = (neighbor * 8 + edge_of * 2 + reverse).reshape(-1)
    row = jnp.arange(SHARE, dtype=jnp.int32)
    rim = onehot(rim_cell(row // EDGE, row // PART % DEPTH, row % PART * SPLIT + part), CELLS)
    targets = jnp.arange(neighbor.shape[0] // columns, dtype=jnp.int32)[:, None] * columns + tile % columns
    fan = jnp.arange(FANS, dtype=jnp.int32)
    nbr, edge, flip = lookup(seams, targets * 4 + fan // 2)
    chain = [(nbr, edge, jnp.broadcast_to(fan % 2, nbr.shape))]
    for j in range(1, DEPTH):
        chain.append(walk(seams, *chain[-1]))
    around, edges, ends = zip(*chain[1:])
    j, c, x = pad_cells(SLOTS, SLOT_ROWS)
    end = spread(ends, j)
    place = x * SPLIT + jnp.where(end == 1, SPLIT - 1 - part, part)
    inner = spread(edges, j) * EDGE + c * PART + jnp.where(end == 1, PART - 1 - x, x)
    inner = jnp.where((j > 0) & (place + j <= DEPTH), inner, -SHARE * columns)
    strip = [nbr[:, 0::2], edge[:, 0::2]]
    strip = [jnp.concatenate([jnp.broadcast_to(v[:, d : d + 1], (v.shape[0], EDGE)) for d in range(4)], 1) for v in strip]
    source = jnp.concatenate([strip[0], spread(around, j).reshape(-1, FANS * SLOT_ROWS)], axis=1)
    place = jnp.concatenate([strip[1] * EDGE + row % EDGE, inner.reshape(-1, FANS * SLOT_ROWS)], axis=1)
    place = jnp.where(source // columns == tile // columns, source % columns * SHARE + place, -1)
    pick = onehot(place.reshape(-1), columns * SHARE)
    mine = (targets == tile).astype(jnp.int32)
    edge, flip = jnp.sum(edge * mine, axis=0)[0::2], jnp.sum(flip * mine, axis=0)[0::2]
    edges = [jnp.sum(v * mine, axis=0) for v in edges]
    ends = [jnp.sum(v * mine, axis=0) for v in ends]
    cells = block_cells(DEPTH)
    j, c, x = pad_cells(cells, FAN_ROWS)
    slot = np.array([SLOTS.index((a, b, d // SPLIT)) for a, b, d in cells] + [0] * (FAN_ROWS - len(cells)), np.int32)
    member = jnp.where(spread(ends, j) == 1, SPLIT - 1 - x % SPLIT, x % SPLIT)
    gather = onehot(jnp.where(j > 0, member * SLOT_ROWS + slot, -1).reshape(-1), SPLIT * SLOT_ROWS)
    taps = [fan_taps(depth, edges, ends) for depth in range(DEPTH, 2, -1)]
    row = np.arange(RING)
    d, place = row // SIDE, row % SIDE
    order = onehot(jnp.asarray(place % SPLIT * 4 * PART + d * PART + place // SPLIT, jnp.int32), RING)
    fan, depth = np.arange(FANS * 8) // 8, np.arange(FANS * 8) % 8
    tips = onehot(jnp.asarray(depth * RING + fan // 2 * SIDE + fan % 2 * (SIDE - 1), jnp.int32), DEPTH * RING)
    end = np.where(place == 0, 0, np.where(place == SIDE - 1, 1, -1))
    target = np.where(end < 0, -1, (d * 2 + end) * 8 + np.arange(DEPTH)[:, None])
    beyond = onehot(jnp.asarray(target.reshape(-1), jnp.int32), FANS * 8)
    flip = jnp.concatenate([jnp.broadcast_to(flip[k : k + 1], (SIDE,)) for k in range(4)])
    turned = jnp.where(flip == 1, SIDE - 1 - place, place)
    facing = onehot(rim_cell(d, 0, turned), CELLS)
    turn = onehot(d * SIDE + turned, RING)
    return edge, rim, pick, (gather, order, tips, beyond, facing, turn, *taps)


def sigmoid(value):
    return 1.0 / (1.0 + jnp.exp(-value))


def fill_patches(state, padded, patches):
    padded[1 : SIDE + 1, 8 : SIDE + 8, :] = (
        state[0:CELLS, :].astype(jnp.float32).reshape(SIDE, SIDE, C)
    )
    halo = state[CELLS : CELLS + RING, :].astype(jnp.float32)
    empty = jnp.zeros((8, C), jnp.float32)
    for row, first in ((0, 0), (SIDE + 1, 2 * SIDE)):
        padded[row, 0:8, :] = empty
        padded[row, 8 : SIDE + 8, :] = halo[first : first + SIDE]
        padded[row, SIDE + 8 : SIDE + 16, :] = empty
    padded[1 : SIDE + 1, SIDE + 8, :] = halo[SIDE : 2 * SIDE]
    padded[1 : SIDE + 1, 7, :] = halo[3 * SIDE : 4 * SIDE]
    for dx in range(3):
        shifted = padded[:, 7 + dx : 7 + dx + SIDE, :].astype(jnp.bfloat16)
        shifted = shifted.reshape((SIDE + 2) * SIDE, C)
        for dy in range(3):
            k = dy * 3 + dx
            patches[:, k * C : (k + 1) * C] = shifted[dy * SIDE : dy * SIDE + CELLS]


def next_state(state, pre_act):
    return (state + pre_act * sigmoid(pre_act)).astype(jnp.bfloat16)


def dot(a, b):
    return jnp.dot(a, b, preferred_element_type=jnp.float32)


def update_strips(edge, strips, ends, mine, weights, side_patches):
    rows = len(strips) - 1
    place = iota((RING, C), 0) % SIDE
    moved = []
    for cells, beyond in [(mine, jnp.zeros_like(mine))] + list(zip(strips, ends)):
        below = jnp.where(place == 0, beyond, pltpu.roll(cells, 1, 0))
        above = jnp.where(place == SIDE - 1, beyond, pltpu.roll(cells, RING - 1, 0))
        moved.append([v.astype(jnp.bfloat16) for v in (below, cells, above)])
    for d in range(4):
        e = edge[d]
        for a in range(3):
            across = jnp.where((e == 0) | (e == 3), a, 2 - a)
            for b in range(3):
                tap = jnp.where(e % 2 == 0, 3 * across + b, 3 * b + across)
                lanes = pl.ds(pl.multiple_of(tap * C, C), C)
                for r in range(rows):
                    first = r * RING + d * SIDE
                    side_patches[first : first + SIDE, lanes] = moved[r + a][b][d * SIDE : (d + 1) * SIDE]
    before = jnp.concatenate(strips[:rows], axis=0)
    after = next_state(before, dot(side_patches[0 : rows * RING, :], weights)).astype(jnp.float32)
    return [after[r * RING : (r + 1) * RING] for r in range(rows)]


def update_fans(taps, fans, tips, weights, fan_patches):
    columns = taps.shape[1]
    rows = taps.shape[0] // (FANS * TAPS)
    centers = []
    for f in range(FANS):
        known = fans[f]
        pool = [known, tips[f * 8 : (f + 1) * 8]]
        spare = columns - known.shape[0] - 8
        if spare:
            pool.append(jnp.zeros((spare, C), jnp.float32))
        pool = jnp.concatenate(pool, axis=0).astype(jnp.bfloat16)
        found = dot(taps[f * TAPS * rows : (f + 1) * TAPS * rows, :], pool)
        for k in range(TAPS):
            fan_patches[f * rows : (f + 1) * rows, k * C : (k + 1) * C] = found[k * rows : (k + 1) * rows].astype(
                jnp.bfloat16
            )
        centers.append(found[4 * rows : 5 * rows])
    pre_act = dot(fan_patches[0 : FANS * rows, :], weights)
    after = next_state(jnp.concatenate(centers, axis=0), pre_act).astype(jnp.float32)
    return [after[f * rows : (f + 1) * rows] for f in range(FANS)]


def sections_kernel(*refs):
    index, edge, start, gathered, weights, gather, order, tips_of, beyond, facing, turn = refs[:11]
    taps, refs = refs[11 : 11 + DEPTH - 2], refs[11 + DEPTH - 2 :]
    kept, sent, states, padded, patches, side_patches, fan_patches, sems = refs

    def deliver(i, act):
        for slot, target in ((0, kept), (1, sent)):

            @pl.when(index[slot] == i)
            def _():
                act(pltpu.make_async_copy(states.at[i], target, sems.at[slot]))

    states[0, 0:CELLS, :] = start[...]
    strips = []
    for r in range(DEPTH):
        found = [
            gathered[q * PICK + d * EDGE + r * PART : q * PICK + d * EDGE + (r + 1) * PART, :].astype(jnp.float32)
            for q in range(SPLIT)
            for d in range(4)
        ]
        strips.append(dot(order[...], jnp.concatenate(found, axis=0).astype(jnp.bfloat16)))
    fans = []
    for f in range(FANS):
        first = SHARE + f * SLOT_ROWS
        found = [
            gathered[q * PICK + first : q * PICK + first + SLOT_ROWS, :].astype(jnp.float32) for q in range(SPLIT)
        ]
        found = jnp.concatenate(found, axis=0).astype(jnp.bfloat16)
        fans.append(dot(gather[f * FAN_ROWS : (f + 1) * FAN_ROWS, :], found))
    for i in range(DEPTH):
        state = states.at[i]
        state[CELLS : CELLS + RING, :] = dot(turn[...], strips[0].astype(jnp.bfloat16)).astype(jnp.bfloat16)
        deliver(i, lambda copy: copy.start())
        if i == DEPTH - 1:
            break
        known = DEPTH - i
        tile = state[0:CELLS, :]
        fill_patches(state, padded, patches)
        outer = jnp.concatenate([fan[0:8] for fan in fans], axis=0).astype(jnp.bfloat16)
        ends = dot(beyond[0 : known * RING, :], outer)
        ends = [ends[r * RING : (r + 1) * RING] for r in range(known)]
        mine = dot(facing[...], tile)
        moved = update_strips(edge, strips, ends, mine, weights[i], side_patches)
        if known > 2:
            cells = round_up(len(block_cells(known)), 8)
            pool = jnp.concatenate([v.astype(jnp.bfloat16) for v in strips], axis=0)
            tips = dot(tips_of[:, 0 : known * RING], pool)
            fans = update_fans(taps[i], [fan[0:cells] for fan in fans], tips, weights[i], fan_patches)
        strips = moved
        states[i + 1, 0:CELLS, :] = next_state(tile.astype(jnp.float32), dot(patches[...], weights[i]))
    for i in range(DEPTH):
        deliver(i, lambda copy: copy.wait())


def all_sections(index, edge, start, gathered, weights, maps):
    vmem = pl.BlockSpec(memory_space=pltpu.VMEM)
    smem = pl.BlockSpec(memory_space=pltpu.SMEM)
    hbm = pl.BlockSpec(memory_space=pl.ANY)
    bf16 = jnp.bfloat16
    state = jax.ShapeDtypeStruct((CELLS + RING, C), bf16)
    fan_rows = FANS * round_up(len(block_cells(DEPTH - 1)), 16)
    return pl.pallas_call(
        sections_kernel,
        out_shape=(state, state),
        in_specs=[smem] * 2 + [vmem] * (3 + len(maps)),
        out_specs=(hbm, hbm),
        scratch_shapes=[
            pltpu.VMEM((DEPTH, CELLS + RING, C), bf16),
            pltpu.VMEM((SIDE + 2, SIDE + 16, C), jnp.float32),
            pltpu.VMEM((CELLS, TAPS * C), bf16),
            pltpu.VMEM(((DEPTH - 1) * RING, TAPS * C), bf16),
            pltpu.VMEM((fan_rows, TAPS * C), bf16),
            pltpu.SemaphoreType.DMA((2,)),
        ],
        compiler_params=pltpu.CompilerParams(vmem_limit_bytes=VMEM_BYTES),
        cost_estimate=pl.CostEstimate(
            flops=3 * DEPTH * CELLS * TAPS * C * C, bytes_accessed=16 << 20, transcendentals=DEPTH * CELLS * C
        ),
        name="all_sections",
    )(index, edge, start, gathered, weights, *maps)


def gradient_kernel(last, index, state, cotangents, weights, before, level, term, padded, patches, cotangent, sem):
    load = pltpu.make_async_copy(cotangents.at[index[0]], cotangent, sem)
    load.start()
    fill_patches(state, padded, patches)
    pre_act = dot(patches[...], weights[...])
    load.wait()
    gate = sigmoid(pre_act)
    level[...] = (state[0:CELLS, :].astype(jnp.float32) + pre_act * gate).astype(jnp.bfloat16)
    slope = gate * (1.0 + pre_act * (1.0 - gate))
    delta = (cotangent[...].astype(jnp.float32) * slope).astype(jnp.bfloat16)
    added = before[...] + lax.dot_general(
        delta, patches[...], (((0,), (0,)), ((), ())), preferred_element_type=jnp.float32
    )
    if not last:
        term[...] = added
        return
    for k in range(TAPS):
        term[k * C : (k + 1) * C, :] = added[:, k * C : (k + 1) * C].T.astype(jnp.bfloat16)


def gradient(sample, state, cotangents, weights, before, last):
    vmem = pl.BlockSpec(memory_space=pltpu.VMEM)
    smem = pl.BlockSpec(memory_space=pltpu.SMEM)
    hbm = pl.BlockSpec(memory_space=pltpu.HBM)
    return pl.pallas_call(
        lambda *refs: gradient_kernel(last, *refs),
        out_shape=(
            jax.ShapeDtypeStruct((CELLS, C), jnp.bfloat16),
            jax.ShapeDtypeStruct((TAPS * C, C), jnp.bfloat16) if last else jax.ShapeDtypeStruct((C, TAPS * C), jnp.float32),
        ),
        in_specs=[smem, vmem, hbm, vmem, vmem],
        out_specs=(vmem,) * 2,
        scratch_shapes=[
            pltpu.VMEM((SIDE + 2, SIDE + 16, C), jnp.float32),
            pltpu.VMEM((CELLS, TAPS * C), jnp.bfloat16),
            pltpu.VMEM((CELLS, C), jnp.bfloat16),
            pltpu.SemaphoreType.DMA,
        ],
        compiler_params=pltpu.CompilerParams(vmem_limit_bytes=VMEM_BYTES),
        cost_estimate=pl.CostEstimate(
            flops=2 * 2 * CELLS * TAPS * C * C, bytes_accessed=3 << 20, transcendentals=CELLS * C
        ),
        name="gradient",
    )(sample, state, cotangents, weights, before)


def add_parts_kernel(parts, out):
    total = parts[0].astype(jnp.float32)
    for i in range(1, parts.shape[0]):
        total = total + parts[i].astype(jnp.float32)
    out[...] = total.astype(out.dtype)


def add_parts(parts):
    vmem = pl.BlockSpec(memory_space=pltpu.VMEM)
    return pl.pallas_call(
        add_parts_kernel,
        out_shape=jax.ShapeDtypeStruct(parts.shape[1:], parts.dtype),
        in_specs=[vmem],
        out_specs=vmem,
        compiler_params=pltpu.CompilerParams(vmem_limit_bytes=4 * 1024 * 1024),
        cost_estimate=pl.CostEstimate(flops=parts.size, bytes_accessed=4 * parts.size, transcendentals=0),
        name="add_parts",
    )(parts)


def share_out(block, axis, groups=None):
    count = lax.axis_size(axis) if groups is None else len(groups[0])
    return lax.all_to_all(
        jnp.broadcast_to(block[None], (count,) + block.shape), axis, 0, 0, axis_index_groups=groups
    )


def sum_terms(term):
    count = lax.axis_size("tile")
    rows = term.shape[0] // count
    pieces = lax.all_to_all(term.reshape(count, rows, term.shape[1]), "tile", 0, 0)
    piece = jnp.sum(pieces.astype(jnp.float32), axis=0).astype(jnp.bfloat16)
    pieces = share_out(piece, ("dp", "tile")).reshape((lax.axis_size("dp"),) + term.shape)
    return jnp.sum(pieces.astype(jnp.float32), axis=0)


def local(inputs, neighbor, edge_of, reverse, weights, cotangent):
    segment = lax.axis_index("segment")
    sample, part = segment // SPLIT, segment % SPLIT
    partner = segment ^ SPLIT
    teams = [[t * SPLIT + p for p in range(SPLIT)] for t in range(2)]
    kernels = lax.all_gather(weights, "segment", axis=0, tiled=True)
    tiles = neighbor.shape[0]
    rows = 4 if tiles % 8 == 0 else 2
    columns = tiles // rows
    along_row = [[r * columns + c for c in range(columns)] for r in range(rows)]
    along_column = [[r * columns + c for r in range(rows)] for c in range(columns)]
    edge, rim, pick, maps = selections(neighbor, edge_of, reverse, lax.axis_index("tile"), part, columns)
    index = jnp.stack([segment, partner]).astype(jnp.int32)
    state = lax.dynamic_index_in_dim(inputs[:, 0], sample, 0, False).reshape(CELLS, C)
    share = dot(rim, state).astype(jnp.bfloat16)
    rims = share_out(share, "tile", along_row).reshape(-1, C)
    picked = dot(pick, rims).astype(jnp.bfloat16).reshape(rows, PICK, C)
    picked = lax.all_to_all(picked, "tile", 0, 0, axis_index_groups=along_column)
    picked = add_parts(picked)
    gathered = lax.all_gather(picked, "segment", axis=0, tiled=True, axis_index_groups=teams)
    kept, sent = all_sections(index, edge, state, gathered, kernels, maps)
    other = lax.ppermute(sent, "segment", [(s, s ^ SPLIT) for s in range(8)])
    cotans = cotangent[0, :, 0].reshape(2, CELLS, C)
    mine, theirs = sample.reshape(1).astype(jnp.int32), (1 - sample).reshape(1).astype(jnp.int32)
    zero = jnp.zeros((C, TAPS * C), jnp.float32)
    level_mine, term = gradient(mine, kept, cotans, weights[0], zero, False)
    level_other, term = gradient(theirs, other, cotans, weights[0], term, True)
    total = sum_terms(term)
    low = jnp.where(sample == 0, level_mine, level_other)
    high = jnp.where(sample == 0, level_other, level_mine)
    levels = jnp.stack([low, high]).reshape(1, 2, 1, SIDE, SIDE, C)
    return levels, total[None]


def solution(mesh):
    placed = (
        P("dp", "tile", None, None, None),
        P(),
        P(),
        P(),
        P("segment", None, None),
        P("segment", "dp", "tile", None, None, None),
    )
    return jax.shard_map(
        local,
        mesh=mesh,
        in_specs=placed,
        out_specs=(P("segment", "dp", "tile", None, None, None), P("segment", None, None)),
        check_vma=False,
    )
```

```python
import jax
import jax.numpy as jnp
import numpy as np
from jax import lax
from jax.experimental import pallas as pl
from jax.experimental.pallas import tpu as pltpu
from jax.sharding import PartitionSpec as P

SIDE = 32
CELLS = SIDE * SIDE
RING = 4 * SIDE
C = 128
TAPS = 9
DEPTH = 8
SPLIT = 4
PART = SIDE // SPLIT
EDGE = DEPTH * PART
SHARE = 4 * EDGE
FANS = 8
VMEM_BYTES = 60 * 1024 * 1024
GRADIENT_VMEM_BYTES = 20 * 1024 * 1024


def round_up(value, step):
    return -(-value // step) * step


def block_cells(depth):
    return [
        (j, c, x) for j in range(1, depth) for c in range(depth - j) for x in range(depth - j + 1)
    ]


SLOTS = [(j, c, x) for j in range(1, DEPTH) for c in range(DEPTH - j) for x in range((DEPTH - j) // SPLIT + 1)]
SLOT_ROWS = round_up(len(SLOTS), 8)
PICK = SHARE + FANS * SLOT_ROWS
FAN_ROWS = round_up(len(block_cells(DEPTH)) + 8, 16)
BLOCKS = DEPTH - 1


def fan_layout(depth):
    step = 1 if depth == DEPTH else 16
    rows, starts = {}, [0]
    for j in range(1, depth):
        block = [cell for cell in block_cells(depth) if cell[0] == j]
        rows.update({cell: starts[-1] + n for n, cell in enumerate(block)})
        starts.append(round_up(starts[-1] + len(block), step))
    return rows, starts, round_up(starts[-1], 8)


def fan_taps(depth):
    source, _, after = fan_layout(depth)
    target, _, rows = fan_layout(depth - 1)
    table = np.zeros((TAPS * rows, round_up(after + 8, 16)), np.float32)
    for (j, c, x), row in target.items():
        for down in (-1, 0, 1):
            for along in (-1, 0, 1):
                deep, place = c + down, x + along
                if deep < 0 and place < 0:
                    continue
                if deep >= 0 and place >= 0:
                    column = source[j, deep, place]
                elif place < 0:
                    column = source[j + 1, 0, deep]
                else:
                    column = after + place if j == 1 else source[j - 1, place, 0]
                table[((down + 1) * 3 + along + 1) * rows + row, column] = 1
    return table


def member_rows(end):
    table = np.zeros((FAN_ROWS, SPLIT * SLOT_ROWS), np.float32)
    for (j, c, x), row in fan_layout(DEPTH)[0].items():
        member = SPLIT - 1 - x % SPLIT if end else x % SPLIT
        table[row, member * SLOT_ROWS + SLOTS.index((j, c, x // SPLIT))] = 1
    return table


def constant_maps():
    row = np.arange(RING)
    d, place = row // SIDE, row % SIDE
    order = np.zeros((RING, RING), np.float32)
    order[row, place % SPLIT * 4 * PART + d * PART + place // SPLIT] = 1
    tips = np.zeros((FANS * 8, DEPTH * RING), np.float32)
    beyond = np.zeros((DEPTH * RING, FANS * 8), np.float32)
    for fan in range(FANS):
        for depth in range(DEPTH):
            column = depth * RING + fan // 2 * SIDE + fan % 2 * (SIDE - 1)
            tips[fan * 8 + depth, column] = 1
            beyond[column, fan * 8 + depth] = 1
    taps = [fan_taps(depth) for depth in range(DEPTH, 2, -1)]
    tables = [order, tips, beyond, member_rows(0), member_rows(1), *taps]
    return [jnp.asarray(table.astype(jnp.bfloat16)) for table in tables]


def iota(shape, axis):
    return lax.broadcasted_iota(jnp.int32, shape, axis)


def onehot(target, columns):
    return (target[:, None] == iota((target.shape[0], columns), 1)).astype(jnp.bfloat16)


def lookup(seams, slot):
    hit = slot[..., None] == jnp.arange(seams.shape[0], dtype=jnp.int32)
    found = jnp.sum(jnp.where(hit, seams, 0), axis=-1)
    return found // 8, found // 2 % 4, found % 2


def rim_cell(edge, depth, place):
    last = SIDE - 1
    return jnp.where(
        edge == 0,
        depth * SIDE + place,
        jnp.where(
            edge == 1,
            place * SIDE + last - depth,
            jnp.where(edge == 2, (last - depth) * SIDE + place, place * SIDE + depth),
        ),
    )


def walk(seams, tile, edge, end):
    corner = jnp.where((edge == 0) | (edge == 3), 0, 1)
    tile, edge, flip = lookup(seams, tile * 4 + jnp.where(edge % 2 == 0, 3 - 2 * end, 2 * end))
    return tile, edge, jnp.where(flip == 1, 1 - corner, corner)


def spread(columns, steps):
    return sum(jnp.where(steps == j, column[..., None], 0) for j, column in enumerate(columns, 1))


def pad_cells(cells, count):
    cells = cells + [(0, 0, 0)] * (count - len(cells))
    return [np.array(column, np.int32) for column in zip(*cells)]


def selections(neighbor, edge_of, reverse, tile, part, columns):
    seams = (neighbor * 8 + edge_of * 2 + reverse).reshape(-1)
    row = jnp.arange(SHARE, dtype=jnp.int32)
    rim = onehot(rim_cell(row // EDGE, row // PART % DEPTH, row % PART * SPLIT + part), CELLS)
    targets = jnp.arange(neighbor.shape[0] // columns, dtype=jnp.int32)[:, None] * columns + tile % columns
    fan = jnp.arange(FANS, dtype=jnp.int32)
    nbr, edge, flip = lookup(seams, targets * 4 + fan // 2)
    chain = [(nbr, edge, jnp.broadcast_to(fan % 2, nbr.shape))]
    for j in range(1, DEPTH):
        chain.append(walk(seams, *chain[-1]))
    around, edges, ends = zip(*chain[1:])
    j, c, x = pad_cells(SLOTS, SLOT_ROWS)
    end = spread(ends, j)
    place = x * SPLIT + jnp.where(end == 1, SPLIT - 1 - part, part)
    inner = spread(edges, j) * EDGE + c * PART + jnp.where(end == 1, PART - 1 - x, x)
    inner = jnp.where((j > 0) & (place + j <= DEPTH), inner, -SHARE * columns)
    strip = [sum(jnp.where(row // EDGE == d, v[:, 2 * d : 2 * d + 1], 0) for d in range(4)) for v in (nbr, edge)]
    source = jnp.concatenate([strip[0], spread(around, j).reshape(-1, FANS * SLOT_ROWS)], axis=1)
    place = jnp.concatenate([strip[1] * EDGE + row % EDGE, inner.reshape(-1, FANS * SLOT_ROWS)], axis=1)
    place = jnp.where(source // columns == tile // columns, source % columns * SHARE + place, -1)
    pick = onehot(place.reshape(-1), columns * SHARE)
    return rim, pick, (targets, edge, flip, edges, ends)


def own_selections(tile, targets, edge, flip, edges, ends):
    mine = (targets == tile).astype(jnp.int32)
    edge, flip = jnp.sum(edge * mine, axis=0)[0::2], jnp.sum(flip * mine, axis=0)[0::2]
    edges = [jnp.sum(v * mine, axis=0) for v in edges]
    ends = [jnp.sum(v * mine, axis=0) for v in ends]
    d, place = jnp.arange(RING, dtype=jnp.int32) // SIDE, jnp.arange(RING, dtype=jnp.int32) % SIDE
    flip = sum(jnp.where(d == k, flip[k], 0) for k in range(4))
    turned = jnp.where(flip == 1, SIDE - 1 - place, place)
    facing = onehot(rim_cell(d, 0, turned), CELLS)
    turn = onehot(d * SIDE + turned, RING)
    edges, ends = jnp.stack(edges, axis=1), jnp.stack(ends, axis=1)
    down = jnp.where(edges % 2 == 0, 3, 1) * jnp.where((edges == 0) | (edges == 3), 1, -1)
    along = jnp.where(edges % 2 == 0, 1, 3) * jnp.where(ends == 1, -1, 1)
    return jnp.concatenate([edge] + [v.reshape(-1) for v in (down, along, ends)]), (facing, turn)


def sigmoid(value):
    return 1.0 / (1.0 + jnp.exp(-value))


def fill_patches(state, padded, patches):
    padded[1 : SIDE + 1, 8 : SIDE + 8, :] = (
        state[0:CELLS, :].astype(jnp.float32).reshape(SIDE, SIDE, C)
    )
    halo = state[CELLS : CELLS + RING, :].astype(jnp.float32)
    empty = jnp.zeros((8, C), jnp.float32)
    for row, first in ((0, 0), (SIDE + 1, 2 * SIDE)):
        padded[row, 0:8, :] = empty
        padded[row, 8 : SIDE + 8, :] = halo[first : first + SIDE]
        padded[row, SIDE + 8 : SIDE + 16, :] = empty
    padded[1 : SIDE + 1, SIDE + 8, :] = halo[SIDE : 2 * SIDE]
    padded[1 : SIDE + 1, 7, :] = halo[3 * SIDE : 4 * SIDE]
    for dx in range(3):
        shifted = padded[:, 7 + dx : 7 + dx + SIDE, :].astype(jnp.bfloat16)
        shifted = shifted.reshape((SIDE + 2) * SIDE, C)
        for dy in range(3):
            k = dy * 3 + dx
            patches[:, k * C : (k + 1) * C] = shifted[dy * SIDE : dy * SIDE + CELLS]


def next_state(state, pre_act):
    return (state + pre_act * sigmoid(pre_act)).astype(jnp.bfloat16)


def dot(a, b):
    return jnp.dot(a, b, preferred_element_type=jnp.float32)


def update_strips(seams, strips, ends, mine, weights, side_patches):
    rows = len(strips) - 1
    place = iota((RING, C), 0) % SIDE
    moved = []
    for cells, beyond in [(mine, jnp.zeros_like(mine))] + list(zip(strips, ends)):
        below = jnp.where(place == 0, beyond, pltpu.roll(cells, 1, 0))
        above = jnp.where(place == SIDE - 1, beyond, pltpu.roll(cells, RING - 1, 0))
        moved.append([v.astype(jnp.bfloat16) for v in (below, cells, above)])
    for d in range(4):
        e = seams[2 + d]
        for a in range(3):
            across = jnp.where((e == 0) | (e == 3), a, 2 - a)
            for b in range(3):
                tap = jnp.where(e % 2 == 0, 3 * across + b, 3 * b + across)
                lanes = pl.ds(pl.multiple_of(tap * C, C), C)
                for r in range(rows):
                    first = r * RING + d * SIDE
                    side_patches[first : first + SIDE, lanes] = moved[r + a][b][d * SIDE : (d + 1) * SIDE]
    before = jnp.concatenate(strips[:rows], axis=0)
    after = next_state(before, dot(side_patches[0 : rows * RING, :], weights)).astype(jnp.float32)
    return [after[r * RING : (r + 1) * RING] for r in range(rows)]


def update_fans(seams, depth, taps, fans, tips, weights, fan_patches):
    columns = taps.shape[1]
    _, starts, rows = fan_layout(depth - 1)
    centers = []
    for f in range(FANS):
        known = fans[f]
        pool = [known, tips[f * 8 : (f + 1) * 8]]
        spare = columns - known.shape[0] - 8
        if spare:
            pool.append(jnp.zeros((spare, C), jnp.float32))
        pool = jnp.concatenate(pool, axis=0).astype(jnp.bfloat16)
        found = dot(taps[...], pool)
        moved = found.astype(jnp.bfloat16)
        for j in range(depth - 2):
            down, along = seams[6 + f * BLOCKS + j], seams[6 + (FANS + f) * BLOCKS + j]
            first, last = starts[j], starts[j + 1]
            for tap in range(TAPS):
                to = 4 + (tap // 3 - 1) * down + (tap % 3 - 1) * along
                lanes = pl.ds(pl.multiple_of(to * C, C), C)
                fan_patches[f * rows + first : f * rows + last, lanes] = moved[tap * rows + first : tap * rows + last]
        centers.append(found[4 * rows : 5 * rows])
    pre_act = dot(fan_patches[0 : FANS * rows, :], weights)
    after = next_state(jnp.concatenate(centers, axis=0), pre_act).astype(jnp.float32)
    return [after[f * rows : (f + 1) * rows] for f in range(FANS)]


def sections_kernel(*refs):
    count = 10 + DEPTH - 2
    seams, sources, refs = refs[0], refs[1 : 1 + count], refs[1 + count :]
    (kept, sent), held, refs = refs[:2], refs[2 : 2 + count], refs[2 + count :]
    states, padded, patches, side_patches, fan_patches, load_sems, sems = refs
    loads = [pltpu.make_async_copy(a, b, load_sems.at[n]) for n, (a, b) in enumerate(zip(sources, held))]
    for load in loads:
        load.start()
    for load in loads[:9]:
        load.wait()
    start, gathered, facing, turn, order, tips_of, beyond, entered_low, entered_high, weights, *taps = held

    def deliver(i, act):
        for slot, target in ((0, kept), (1, sent)):

            @pl.when(seams[slot] == i)
            def _():
                act(pltpu.make_async_copy(states.at[i], target, sems.at[slot]))

    states[0, 0:CELLS, :] = start[...]
    strips = []
    for r in range(DEPTH):
        found = [
            gathered[q * PICK + d * EDGE + r * PART : q * PICK + d * EDGE + (r + 1) * PART, :].astype(jnp.float32)
            for q in range(SPLIT)
            for d in range(4)
        ]
        strips.append(dot(order[...], jnp.concatenate(found, axis=0).astype(jnp.bfloat16)))
    fans, starts = [], fan_layout(DEPTH)[1]
    for f in range(FANS):
        first = SHARE + f * SLOT_ROWS
        found = [
            gathered[q * PICK + first : q * PICK + first + SLOT_ROWS, :].astype(jnp.float32) for q in range(SPLIT)
        ]
        found = jnp.concatenate(found, axis=0).astype(jnp.bfloat16)
        low, high = dot(entered_low[...], found), dot(entered_high[...], found)
        row = iota((FAN_ROWS, C), 0)
        end = jnp.zeros((FAN_ROWS, C), jnp.int32)
        for j in range(BLOCKS):
            end = jnp.where(row >= starts[j], seams[6 + (2 * FANS + f) * BLOCKS + j], end)
        fans.append(jnp.where(end == 1, high, low))
    for i in range(DEPTH):
        state = states.at[i]
        state[CELLS : CELLS + RING, :] = dot(turn[...], strips[0].astype(jnp.bfloat16)).astype(jnp.bfloat16)
        deliver(i, lambda copy: copy.start())
        if i == DEPTH - 1:
            break
        known = DEPTH - i
        tile = state[0:CELLS, :]
        fill_patches(state, padded, patches)
        if i == 0:
            loads[9].wait()
        outer = jnp.concatenate([fan[0:8] for fan in fans], axis=0).astype(jnp.bfloat16)
        ends = dot(beyond[0 : known * RING, :], outer)
        ends = [ends[r * RING : (r + 1) * RING] for r in range(known)]
        mine = dot(facing[...], tile)
        moved = update_strips(seams, strips, ends, mine, weights[i], side_patches)
        if known > 2:
            cells = fan_layout(known)[2]
            pool = jnp.concatenate([v.astype(jnp.bfloat16) for v in strips], axis=0)
            tips = dot(tips_of[:, 0 : known * RING], pool)
            loads[10 + i].wait()
            fans = update_fans(seams, known, taps[i], [fan[0:cells] for fan in fans], tips, weights[i], fan_patches)
        strips = moved
        states[i + 1, 0:CELLS, :] = next_state(tile.astype(jnp.float32), dot(patches[...], weights[i]))
    for i in range(DEPTH):
        deliver(i, lambda copy: copy.wait())


def all_sections(seams, start, gathered, weights, maps):
    smem = pl.BlockSpec(memory_space=pltpu.SMEM)
    hbm = pl.BlockSpec(memory_space=pl.ANY)
    bf16 = jnp.bfloat16
    fixed = constant_maps()
    arrays = [start, gathered, *maps, *fixed[:5], weights, *fixed[5:]]
    state = jax.ShapeDtypeStruct((CELLS + RING, C), bf16)
    fan_rows = FANS * fan_layout(DEPTH - 1)[2]
    return pl.pallas_call(
        sections_kernel,
        out_shape=(state, state),
        in_specs=[smem] + [hbm] * len(arrays),
        out_specs=(hbm, hbm),
        scratch_shapes=[pltpu.VMEM(a.shape, a.dtype) for a in arrays]
        + [
            pltpu.VMEM((DEPTH, CELLS + RING, C), bf16),
            pltpu.VMEM((SIDE + 2, SIDE + 16, C), jnp.float32),
            pltpu.VMEM((CELLS, TAPS * C), bf16),
            pltpu.VMEM(((DEPTH - 1) * RING, TAPS * C), bf16),
            pltpu.VMEM((fan_rows, TAPS * C), bf16),
            pltpu.SemaphoreType.DMA((len(arrays),)),
            pltpu.SemaphoreType.DMA((2,)),
        ],
        compiler_params=pltpu.CompilerParams(vmem_limit_bytes=VMEM_BYTES),
        cost_estimate=pl.CostEstimate(
            flops=3 * DEPTH * CELLS * TAPS * C * C, bytes_accessed=16 << 20, transcendentals=DEPTH * CELLS * C
        ),
        name="all_sections",
    )(seams, *arrays)


def gradient_kernel(last, index, state, cotangents, weights, before, level, term, padded, patches, cotangent, sem):
    load = pltpu.make_async_copy(cotangents.at[index[0]], cotangent, sem)
    load.start()
    fill_patches(state, padded, patches)
    pre_act = dot(patches[...], weights[...])
    load.wait()
    gate = sigmoid(pre_act)
    level[...] = (state[0:CELLS, :].astype(jnp.float32) + pre_act * gate).astype(jnp.bfloat16)
    slope = gate * (1.0 + pre_act * (1.0 - gate))
    delta = (cotangent[...].astype(jnp.float32) * slope).astype(jnp.bfloat16)
    added = before[...] + lax.dot_general(
        delta, patches[...], (((0,), (0,)), ((), ())), preferred_element_type=jnp.float32
    )
    if not last:
        term[...] = added
        return
    for k in range(TAPS):
        term[k * C : (k + 1) * C, :] = added[:, k * C : (k + 1) * C].T.astype(jnp.bfloat16)


def gradient(sample, state, cotangents, weights, before, last):
    vmem = pl.BlockSpec(memory_space=pltpu.VMEM)
    smem = pl.BlockSpec(memory_space=pltpu.SMEM)
    hbm = pl.BlockSpec(memory_space=pltpu.HBM)
    return pl.pallas_call(
        lambda *refs: gradient_kernel(last, *refs),
        out_shape=(
            jax.ShapeDtypeStruct((CELLS, C), jnp.bfloat16),
            jax.ShapeDtypeStruct((TAPS * C, C), jnp.bfloat16) if last else jax.ShapeDtypeStruct((C, TAPS * C), jnp.float32),
        ),
        in_specs=[smem, vmem, hbm, vmem, vmem],
        out_specs=(vmem,) * 2,
        scratch_shapes=[
            pltpu.VMEM((SIDE + 2, SIDE + 16, C), jnp.float32),
            pltpu.VMEM((CELLS, TAPS * C), jnp.bfloat16),
            pltpu.VMEM((CELLS, C), jnp.bfloat16),
            pltpu.SemaphoreType.DMA,
        ],
        compiler_params=pltpu.CompilerParams(vmem_limit_bytes=GRADIENT_VMEM_BYTES),
        cost_estimate=pl.CostEstimate(
            flops=2 * 2 * CELLS * TAPS * C * C, bytes_accessed=3 << 20, transcendentals=CELLS * C
        ),
        name="gradient",
    )(sample, state, cotangents, weights, before)


def add_parts_kernel(parts, out):
    total = parts[0].astype(jnp.float32)
    for i in range(1, parts.shape[0]):
        total = total + parts[i].astype(jnp.float32)
    out[...] = total.astype(out.dtype)


def add_parts(parts):
    vmem = pl.BlockSpec(memory_space=pltpu.VMEM)
    return pl.pallas_call(
        add_parts_kernel,
        out_shape=jax.ShapeDtypeStruct(parts.shape[1:], parts.dtype),
        in_specs=[vmem],
        out_specs=vmem,
        compiler_params=pltpu.CompilerParams(vmem_limit_bytes=4 * 1024 * 1024),
        cost_estimate=pl.CostEstimate(flops=parts.size, bytes_accessed=4 * parts.size, transcendentals=0),
        name="add_parts",
    )(parts)


def share_out(block, axis, groups=None):
    count = lax.axis_size(axis) if groups is None else len(groups[0])
    return lax.all_to_all(
        jnp.broadcast_to(block[None], (count,) + block.shape), axis, 0, 0, axis_index_groups=groups
    )


def sum_terms(term):
    count = lax.axis_size("tile")
    rows = term.shape[0] // count
    pieces = lax.all_to_all(term.reshape(count, rows, term.shape[1]), "tile", 0, 0)
    piece = jnp.sum(pieces.astype(jnp.float32), axis=0).astype(jnp.bfloat16)
    pieces = share_out(piece, ("dp", "tile")).reshape((lax.axis_size("dp"),) + term.shape)
    return jnp.sum(pieces.astype(jnp.float32), axis=0)


def local(inputs, neighbor, edge_of, reverse, weights, cotangent):
    segment = lax.axis_index("segment")
    sample, part = segment // SPLIT, segment % SPLIT
    partner = segment ^ SPLIT
    teams = [[t * SPLIT + p for p in range(SPLIT)] for t in range(2)]
    kernels = lax.all_gather(weights, "segment", axis=0, tiled=True)
    tiles = neighbor.shape[0]
    rows = 4 if tiles % 8 == 0 else 2
    columns = tiles // rows
    along_row = [[r * columns + c for c in range(columns)] for r in range(rows)]
    along_column = [[r * columns + c for r in range(rows)] for c in range(columns)]
    tile = lax.axis_index("tile")
    rim, pick, found = selections(neighbor, edge_of, reverse, tile, part, columns)
    seams, maps = own_selections(tile, *found)
    index = jnp.stack([segment, partner]).astype(jnp.int32)
    state = lax.dynamic_index_in_dim(inputs[:, 0], sample, 0, False).reshape(CELLS, C)
    share = dot(rim, state).astype(jnp.bfloat16)
    rims = share_out(share, "tile", along_row).reshape(-1, C)
    picked = dot(pick, rims).astype(jnp.bfloat16).reshape(rows, PICK, C)
    picked = lax.all_to_all(picked, "tile", 0, 0, axis_index_groups=along_column)
    picked = add_parts(picked)
    gathered = lax.all_gather(picked, "segment", axis=0, tiled=True, axis_index_groups=teams)
    kept, sent = all_sections(jnp.concatenate([index, seams]), state, gathered, kernels, maps)
    other = lax.ppermute(sent, "segment", [(s, s ^ SPLIT) for s in range(8)])
    cotans = cotangent[0, :, 0].reshape(2, CELLS, C)
    mine, theirs = sample.reshape(1).astype(jnp.int32), (1 - sample).reshape(1).astype(jnp.int32)
    zero = jnp.zeros((C, TAPS * C), jnp.float32)
    level_mine, term = gradient(mine, kept, cotans, weights[0], zero, False)
    level_other, term = gradient(theirs, other, cotans, weights[0], term, True)
    total = sum_terms(term)
    low = jnp.where(sample == 0, level_mine, level_other)
    high = jnp.where(sample == 0, level_other, level_mine)
    levels = jnp.stack([low, high]).reshape(1, 2, 1, SIDE, SIDE, C)
    return levels, total[None]


def solution(mesh):
    placed = (
        P("dp", "tile", None, None, None),
        P(),
        P(),
        P(),
        P("segment", None, None),
        P("segment", "dp", "tile", None, None, None),
    )
    return jax.shard_map(
        local,
        mesh=mesh,
        in_specs=placed,
        out_specs=(P("segment", "dp", "tile", None, None, None), P("segment", None, None)),
        check_vma=False,
    )
```
